512 devices in a mesh: tm: 32 (over z_hi, y), space: 4 (over z_lo, core), heads: 4 (over x).
Axes of the slice: x: 4, y: 8, z: 8 (z_hi: 4, z_lo: 2; z = z_hi * 2 + z_lo), core: 2. Of those that a mesh axis runs over, the one named last changes fastest.
Arguments:
- query_tiles: bfloat16 [32, 4, 384, 1536], P('tm', 'space', None, 'heads'), may hold values from -6 to 6
- key_tiles: bfloat16 [32, 4, 384, 1536], P('tm', 'space', None, 'heads'), may hold values from -6 to 6
- value_tiles: bfloat16 [32, 4, 384, 1536], P('tm', 'space', None, 'heads'), may hold values from -6 to 6
- grad_output: bfloat16 [32, 4, 384, 1536], P('tm', 'space', None, 'heads'), may hold values from -6 to 6
- log_norm: float32 [32, 4, 12, 384], P('tm', 'space', 'heads'), may hold values from 5 to 6.5
- row_delta: float32 [32, 4, 12, 384], P('tm', 'space', 'heads'), may hold values from -24 to 24
- extents: int32 [32, 4, 3], replicated, may hold values from 0 to 1, as said below
Outputs:
- grad_query: bfloat16 [32, 4, 384, 1536], P('tm', 'space', None, 'heads')
- grad_key: bfloat16 [32, 4, 384, 1536], P('tm', 'space', None, 'heads')
- grad_value: bfloat16 [32, 4, 384, 1536], P('tm', 'space', None, 'heads')
The draws below stay inside these ranges and needn't reach their ends.
Inputs may be any that keep to these rules, and one draw needn't show every extreme that they name: `extents`: in every time tile at least one frame tile has time half-extent 1.
All inputs are finite; a program needn't handle non-finite values.
Results may differ from the reference program's by a relative error of at most 0.0057.
Values may be sent and summed in bfloat16 or wider, within the bound.
No kernel may reach another device: no remote copies, remote signals or barrier semaphores. Data moves between devices by JAX's collectives and lax.ppermute only.
A program may use at most 128 MiB of HBM per device.

```python
import jax
import jax.numpy as jnp
from jax import lax

TILE = 384
HEAD_DIM = 128
HEADS = 12
WIDTH_TILES = 2
CHANNELS = 1536
FRAME_TILES = 4
TIME_TILES = 32
TIME_ALL = 32


def draw_extents(key, part):
    key = jax.random.fold_in(key, 7)
    key_base, key_pick = jax.random.split(key)
    base = jax.random.randint(key_base, (TIME_ALL, FRAME_TILES, 3), 0, 2, dtype=jnp.int32)
    picked = jax.random.randint(key_pick, (TIME_ALL, 1), 0, FRAME_TILES, dtype=jnp.int32)
    forced = (jnp.arange(FRAME_TILES, dtype=jnp.int32)[None, :] == picked).astype(jnp.int32)
    time_column = jnp.maximum(base[:, :, 0], forced)
    return jnp.concatenate([time_column[:, :, None], base[:, :, 1:]], axis=2)


def levels(stream_key, extent, pieces, low, top_value):
    gain = 1.0
    for axis_at, shards_of in pieces:
        heights = jax.random.uniform(jax.random.fold_in(jax.random.fold_in(stream_key, 6), axis_at), (shards_of,), jnp.float32, low / len(pieces), top_value / len(pieces))
        gain = gain * jnp.repeat(jnp.exp(heights), extent[axis_at] // shards_of).reshape((-1,) + (1,) * (len(extent) - 1 - axis_at))
    return gain


def scatter_about(key, shape, scale, reach, cuts=(), held_as=jnp.bfloat16):
    drawn = scale * jax.random.normal(key, shape, jnp.float32)
    if cuts:
        drawn = drawn * levels(key, shape, cuts, -0.22, 0.18)
    return jnp.clip(drawn, -reach, reach).astype(held_as)


def setup_inputs(seed: int = 0) -> dict:
    key_list = jax.random.split(jax.random.key(seed), 8)
    return {
        "query_tiles": scatter_about(key_list[0], (TIME_ALL, FRAME_TILES, TILE, CHANNELS), 1.0, 6.0, ((0, 32), (1, 4), (3, 4))),
        "key_tiles": scatter_about(key_list[1], (TIME_ALL, FRAME_TILES, TILE, CHANNELS), 1.0, 6.0, ((0, 32), (1, 4), (3, 4))),
        "value_tiles": scatter_about(key_list[2], (TIME_ALL, FRAME_TILES, TILE, CHANNELS), 1.0, 6.0, ((0, 32), (1, 4), (3, 4))),
        "grad_output": scatter_about(key_list[3], (TIME_ALL, FRAME_TILES, TILE, CHANNELS), 1.0, 6.0, ((0, 32), (1, 4), (3, 4))),
        "log_norm": jnp.clip(5.0 + 1.5 * jax.random.uniform(key_list[4], (TIME_ALL, FRAME_TILES, HEADS, TILE), jnp.float32) ** levels(key_list[4], (TIME_ALL, FRAME_TILES, HEADS, TILE), ((0, 32), (1, 4), (2, 4)), -0.2, 0.2), 5.0, 6.5),
        "row_delta": scatter_about(key_list[5], (TIME_ALL, FRAME_TILES, HEADS, TILE), 4.0, 24.0, ((0, 32), (1, 4), (2, 4)), jnp.float32),
        "extents": draw_extents(jax.random.fold_in(key_list[7], 71), 0),
    }


def pair_terms(query_row, key_row, value_row, grad_row, norm_row, delta_row, allowed, factor):
    scores = jnp.einsum("wqhd,wkhd->whqk", query_row.astype(jnp.float32), key_row.astype(jnp.float32)) * factor
    attend = allowed[:, None, None, None] * jnp.exp(scores - norm_row[..., None])
    attend_low = lax.optimization_barrier(attend.astype(jnp.bfloat16)).astype(jnp.float32)
    grad_attend = jnp.einsum("wqhd,wkhd->whqk", grad_row.astype(jnp.float32), value_row.astype(jnp.float32))
    grad_scores = lax.optimization_barrier((attend * (grad_attend - delta_row[..., None])).astype(jnp.bfloat16)).astype(jnp.float32)
    query_term = jnp.einsum("whqk,wkhd->wqhd", grad_scores, key_row.astype(jnp.float32)) * factor
    key_term = (jnp.einsum("whqk,wqhd->wkhd", grad_scores, query_row.astype(jnp.float32)) * factor).astype(jnp.bfloat16)
    value_term = jnp.einsum("whqk,wqhd->wkhd", attend_low, grad_row.astype(jnp.float32)).astype(jnp.bfloat16)
    return query_term, key_term, value_term


def reference(query_tiles, key_tiles, value_tiles, grad_output, log_norm, row_delta, extents):
    shape_five = (TIME_ALL, FRAME_TILES, TILE, HEADS, HEAD_DIM)
    factor = HEAD_DIM ** -0.5
    query_grid = query_tiles.reshape(shape_five)
    grad_grid = grad_output.reshape(shape_five)
    padding = ((1, 1), (0, 0), (0, 0), (0, 0), (0, 0))
    key_pad = jnp.pad(key_tiles.reshape(shape_five), padding)
    value_pad = jnp.pad(value_tiles.reshape(shape_five), padding)
    grad_query = jnp.zeros(shape_five, jnp.float32)
    key_total = jnp.zeros(key_pad.shape, jnp.float32)
    value_total = jnp.zeros(key_pad.shape, jnp.float32)
    time_index = jnp.arange(TIME_ALL, dtype=jnp.int32)
    frame_index = jnp.arange(FRAME_TILES, dtype=jnp.int32)
    frame_height = frame_index // WIDTH_TILES
    frame_width = frame_index % WIDTH_TILES
    for step_time in (-1, 0, 1):
        for target in range(FRAME_TILES):
            def one_row(time_pos, step_time=step_time, target=target):
                key_tile = lax.dynamic_index_in_dim(key_pad, time_pos + step_time + 1, 0, keepdims=False)[target]
                value_tile = lax.dynamic_index_in_dim(value_pad, time_pos + step_time + 1, 0, keepdims=False)[target]
                key_row = jnp.broadcast_to(key_tile, (FRAME_TILES,) + key_tile.shape)
                value_row = jnp.broadcast_to(value_tile, (FRAME_TILES,) + value_tile.shape)
                query_row = lax.dynamic_index_in_dim(query_grid, time_pos, 0, keepdims=False)
                grad_row = lax.dynamic_index_in_dim(grad_grid, time_pos, 0, keepdims=False)
                norm_row = lax.dynamic_index_in_dim(log_norm, time_pos, 0, keepdims=False)
                delta_row = lax.dynamic_index_in_dim(row_delta, time_pos, 0, keepdims=False)
                extent_row = lax.dynamic_index_in_dim(extents, time_pos, 0, keepdims=False)
                clip_time = time_pos % TIME_TILES + step_time
                inside = (clip_time >= 0) & (clip_time < TIME_TILES)
                height_gap = jnp.abs(frame_height[target] - frame_height)
                width_gap = jnp.abs(frame_width[target] - frame_width)
                allowed = (inside & (abs(step_time) <= extent_row[:, 0]) & (height_gap <= extent_row[:, 1]) & (width_gap <= extent_row[:, 2])).astype(jnp.float32)
                return pair_terms(query_row, key_row, value_row, grad_row, norm_row, delta_row, allowed, factor)

            query_terms, key_terms, value_terms = lax.map(one_row, time_index)
            grad_query = grad_query + query_terms
            row_lo = step_time + 1
            key_total = key_total.at[row_lo:row_lo + TIME_ALL, target].add(jnp.sum(key_terms.astype(jnp.float32), axis=1))
            value_total = value_total.at[row_lo:row_lo + TIME_ALL, target].add(jnp.sum(value_terms.astype(jnp.float32), axis=1))
    out_shape = (TIME_ALL, FRAME_TILES, TILE, CHANNELS)
    grad_key = key_total[1:-1].astype(jnp.bfloat16).reshape(out_shape)
    grad_value = value_total[1:-1].astype(jnp.bfloat16).reshape(out_shape)
    return grad_query.astype(jnp.bfloat16).reshape(out_shape), grad_key, grad_value
```

```python
import functools

import jax
import jax.numpy as jnp
from jax import lax
from jax.experimental import pallas as pl
from jax.experimental.pallas import tpu as pltpu
from jax.sharding import PartitionSpec as P

RING = 8
LOG2E = 1.4426950408889634
HEAD = 128
BF = jnp.bfloat16
F32 = jnp.float32


def send(block, pairs):
    return lax.ppermute(block, ("tm", "space"), pairs)


def routes(time_all):
    at = lambda t, c, w: t * 4 + c * 2 + w
    ts, cs = range(time_all), range(2)
    core = [(at(t, c, w), at(t, c, 1 - w)) for t in ts for c in cs for w in cs]
    pair = [(at(t, c, w), at(t, 1 - c, w)) for t in ts for c in cs for w in cs]
    up, lend, lent_core = [], [], []
    for t in range(time_all - 1):
        for w in cs:
            if t % RING == RING - 1:
                up.append((at(t, 1, w), at(t + 1, 0, w)))
                lend.append((at(t, 0, w), at(t, 1, w)))
                lend.append((at(t + 1, 1, w), at(t + 1, 0, w)))
                lent_core.append((at(t, 1, w), at(t, 1, 1 - w)))
                lent_core.append((at(t + 1, 0, w), at(t + 1, 0, 1 - w)))
            else:
                up += [(at(t, c, w), at(t + 1, c, w)) for c in cs]
    back = lambda pairs: [(j, i) for i, j in pairs]
    return dict(core=core, pair=pair, up=up, down=back(up), lend=lend, lent_core=lent_core, give=back(lend))


def aux_rows(pack, rows):
    return pack[2 * rows :, :].astype(F32)


def accumulate(pack, flags, base, count, kv, acc, dq, rows, factor):
    heads = pack.shape[1] // HEAD
    dq[...] = jnp.zeros_like(dq)
    aux = pack[2 * rows :, :].astype(F32)

    def step(j, carry):
        @pl.when(flags[base + j] != 0)
        def _():
            for h in range(heads):
                cols = slice(h * HEAD, (h + 1) * HEAD)
                part = lambda i: aux[(3 * i) * heads + h : (3 * i) * heads + h + 1] + (
                    aux[(3 * i + 1) * heads + h : (3 * i + 1) * heads + h + 1]
                    + aux[(3 * i + 2) * heads + h : (3 * i + 2) * heads + h + 1]
                )
                norm, delta = part(0) * LOG2E, part(1)
                q, g = pack[0:rows, cols], pack[rows : 2 * rows, cols]
                k, v = kv[j, 0:rows, cols], kv[j, rows : 2 * rows, cols]
                last = (((1,), (1,)), ((), ()))
                st = lax.dot_general(k, q, last, preferred_element_type=F32)
                p = jnp.exp2(st * (factor * LOG2E) - norm)
                dp = lax.dot_general(v, g, last, preferred_element_type=F32)
                ds = (p * (dp - delta)).astype(BF)
                acc[j, rows : 2 * rows, cols] += jnp.dot(p.astype(BF), g, preferred_element_type=F32)
                acc[j, 0:rows, cols] += jnp.dot(ds, q, preferred_element_type=F32)
                dq[:, cols] += lax.dot_general(ds, k, (((0,), (0,)), ((), ())), preferred_element_type=F32)

        return carry

    lax.fori_loop(0, count, step, 0)


def frame_kernel(rows, factor, flags, mine, other, kv_a, kv_b, acc, dq_mine, dq_other, kv):
    kv[0] = kv_a[...]
    kv[1] = kv_b[...]
    acc[...] = jnp.zeros_like(acc)
    accumulate(mine, flags, 0, 2, kv, acc, dq_mine, rows, factor)
    accumulate(other, flags, 4, 2, kv, acc, dq_other, rows, factor)
    dq_mine[...] = dq_mine[...] * factor
    dq_other[...] = dq_other[...] * factor


def near_kernel(rows, factor, flags, low, high, kv_a, kv_b, kv_c, kv_d, acc_in, acc, dq_low, dq_high, kv, dq):
    for i, ref in enumerate((kv_a, kv_b, kv_c, kv_d)):
        kv[i] = ref[...]
    acc[0:2] = acc_in[...]
    acc[2:4] = jnp.zeros_like(acc[2:4])
    accumulate(low, flags, 8, 4, kv, acc, dq, rows, factor)
    dq_low[...] = (dq[...] * factor).astype(BF)
    accumulate(high, flags, 12, 4, kv, acc, dq, rows, factor)
    dq_high[...] = (dq[...] * factor).astype(BF)


def far_kernel(rows, factor, flags, low, high, kv_a, kv_b, kv_c, kv_d, acc_in, near_low, near_high,
               msg_low, msg_high, own, lent, sib, kv, acc, dq):
    for i, ref in enumerate((kv_a, kv_b, kv_c, kv_d)):
        kv[i] = ref[...]
    acc[...] = acc_in[...]
    msg_low[0:rows] = near_low[...]
    msg_high[0:rows] = near_high[...]
    accumulate(low, flags, 16, 4, kv, acc, dq, rows, factor)
    msg_low[rows:] = (dq[...] * factor).astype(BF)
    accumulate(high, flags, 20, 4, kv, acc, dq, rows, factor)
    msg_high[rows:] = (dq[...] * factor).astype(BF)
    own[0:rows] = acc[0, 0:rows] * factor
    own[rows:] = acc[0, rows:]
    lent[0:rows] = acc[2, 0:rows] * factor
    lent[rows:] = acc[2, rows:]
    for i, j in enumerate((1, 3)):
        sib[i, 0:rows] = (acc[j, 0:rows] * factor).astype(BF)
        sib[i, rows:] = acc[j, rows:].astype(BF)


def call(kernel, shapes, scratch, operands, pairs, name):
    whole = pl.BlockSpec(memory_space=pltpu.VMEM)
    return pl.pallas_call(
        kernel,
        out_shape=shapes,
        in_specs=[pl.BlockSpec(memory_space=pltpu.SMEM)] + [whole] * (len(operands) - 1),
        out_specs=[whole] * len(shapes),
        scratch_shapes=scratch,
        compiler_params=pltpu.CompilerParams(vmem_limit_bytes=40 * 2**20),
        cost_estimate=pl.CostEstimate(flops=pairs * 566_000_000, bytes_accessed=8_000_000, transcendentals=pairs * 442_368),
        name=name,
    )(*operands)


def thirds(x):
    hi = lax.reduce_precision(x, 8, 7)
    mid = lax.reduce_precision(x - hi, 8, 7)
    return [hi.astype(BF), mid.astype(BF), (x - hi - mid).astype(BF)]


def pair_flags(extents, time_pos, chip, core, time_all):
    low_cross = (time_pos % RING == 0) & (time_pos > 0)
    high_cross = (time_pos % RING == RING - 1) & (time_pos < time_all - 1)
    false = jnp.bool_(False)
    flags = []
    for step, cross, inner, flip in (
        (0, false, false, 0), (0, false, false, 1),
        (-1, low_cross, chip == 0, 0), (1, high_cross, chip == 1, 0),
        (-1, low_cross, chip == 0, 1), (1, high_cross, chip == 1, 1),
    ):
        when = time_pos + step
        inside = (when >= 0) & (when < time_all)
        height = jnp.where(cross, 1 - chip, chip)
        height = 1 - height if flip else height
        extent = extents[jnp.clip(when, 0, time_all - 1), height * 2 + core]
        for key_flip, width_gap in ((0, 0), (0, 1), (1, 0), (1, 1)):
            key_height = 1 - chip if key_flip else chip
            taken = cross & inner if key_flip else ~cross | inner
            flags.append(
                inside & taken & (abs(step) <= extent[0])
                & (jnp.abs(key_height - height) <= extent[1]) & (width_gap <= extent[2])
            )
    return jnp.stack(flags).astype(jnp.int32)


def body(query_tiles, key_tiles, value_tiles, grad_output, log_norm, row_delta, extents):
    rows, channels = query_tiles.shape[2:]
    heads = log_norm.shape[2]
    factor = (channels // heads) ** (-0.5)
    time_all = lax.axis_size("tm")
    time_pos, frame_pos = lax.axis_index("tm"), lax.axis_index("space")
    chip, core = frame_pos // 2, frame_pos % 2
    route = routes(time_all)
    flags = pair_flags(extents, time_pos, chip, core, time_all)

    pad = jnp.zeros((32 - 6 * heads, channels), BF)
    mine = jnp.concatenate(
        [query_tiles[0, 0], grad_output[0, 0]] + thirds(log_norm[0, 0]) + thirds(row_delta[0, 0]) + [pad]
    )
    kv_a = jnp.concatenate([key_tiles[0, 0], value_tiles[0, 0]])

    other = send(mine, route["pair"])
    near_low = send(mine, route["up"])
    near_high = send(mine, route["down"])
    kv_b = send(kv_a, route["core"])
    far_low = send(other, route["up"])
    far_high = send(other, route["down"])
    kv_c = send(kv_a, route["lend"])
    kv_d = send(kv_c, route["lent_core"])

    tile, two = (rows, channels), (2 * rows, channels)
    out = jax.ShapeDtypeStruct
    with jax.named_scope("frame"):
        acc, dq_mine, dq_other = call(
            functools.partial(frame_kernel, rows, factor),
            [out((2,) + two, F32), out(tile, F32), out(tile, F32)],
            [pltpu.VMEM((2,) + two, BF)],
            (flags, mine, other, kv_a, kv_b), 4, "frame",
        )
    with jax.named_scope("near"):
        acc, dq_low, dq_high = call(
            functools.partial(near_kernel, rows, factor),
            [out((4,) + two, F32), out(tile, BF), out(tile, BF)],
            [pltpu.VMEM((4,) + two, BF), pltpu.VMEM(tile, F32)],
            (flags, near_low, near_high, kv_a, kv_b, kv_c, kv_d, acc), 6, "near",
        )
    with jax.named_scope("far"):
        msg_low, msg_high, own, lent, sib = call(
            functools.partial(far_kernel, rows, factor),
            [out(two, BF), out(two, BF), out(two, F32), out(two, F32), out((2,) + two, BF)],
            [pltpu.VMEM((4,) + two, BF), pltpu.VMEM((4,) + two, F32), pltpu.VMEM(tile, F32)],
            (flags, far_low, far_high, kv_a, kv_b, kv_c, kv_d, acc, dq_low, dq_high), 6, "far",
        )
    from_high = send(msg_low, route["down"])
    from_low = send(msg_high, route["up"])
    sib = send(sib, route["core"])
    lent = (lent + sib[1].astype(F32)).astype(BF)
    given = send(lent, route["give"])
    other_total = dq_other + from_high[rows:].astype(F32) + from_low[rows:].astype(F32)
    swapped = send(other_total.astype(BF), route["pair"])
    total = dq_mine + from_high[:rows].astype(F32) + from_low[:rows].astype(F32) + swapped.astype(F32)
    grad_kv = (own + sib[0].astype(F32) + given.astype(F32)).astype(BF)
    shape = (1, 1, rows, channels)
    return total.astype(BF).reshape(shape), grad_kv[:rows].reshape(shape), grad_kv[rows:].reshape(shape)


def solution(mesh):
    tiles, per_row = P("tm", "space", None, "heads"), P("tm", "space", "heads", None)
    return jax.shard_map(
        body,
        mesh=mesh,
        in_specs=(tiles, tiles, tiles, tiles, per_row, per_row, P()),
        out_specs=(tiles, tiles, tiles),
        check_vma=False,
    )
```

```python
import functools

import jax
import jax.numpy as jnp
from jax import lax
from jax.experimental import pallas as pl
from jax.experimental.pallas import tpu as pltpu
from jax.sharding import PartitionSpec as P

RING = 8
LOG2E = 1.4426950408889634
HEAD = 128
BF = jnp.bfloat16
F32 = jnp.float32


def send(block, pairs):
    return lax.ppermute(block, ("tm", "space"), pairs)


def routes(time_all):
    at = lambda t, c, w: t * 4 + c * 2 + w
    ts, cs = range(time_all), range(2)
    core = [(at(t, c, w), at(t, c, 1 - w)) for t in ts for c in cs for w in cs]
    pair = [(at(t, c, w), at(t, 1 - c, w)) for t in ts for c in cs for w in cs]
    up, lend, lent_core = [], [], []
    for t in range(time_all - 1):
        for w in cs:
            if t % RING == RING - 1:
                up.append((at(t, 1, w), at(t + 1, 0, w)))
                lend.append((at(t, 0, w), at(t, 1, w)))
                lend.append((at(t + 1, 1, w), at(t + 1, 0, w)))
                lent_core.append((at(t, 1, w), at(t, 1, 1 - w)))
                lent_core.append((at(t + 1, 0, w), at(t + 1, 0, 1 - w)))
            else:
                up += [(at(t, c, w), at(t + 1, c, w)) for c in cs]
    back = lambda pairs: [(j, i) for i, j in pairs]
    across = lambda pairs: [(j, i ^ 2) for i, j in pairs]
    return dict(
        core=core, pair=pair, up=up, down=back(up), lend=lend, lent_core=lent_core, give=back(lend),
        far_down=across(up), far_up=across(back(up)),
    )


def accumulate(pack, flag, count, kv, acc, dq, rows, factor):
    heads = pack.shape[1] // HEAD
    dq[...] = jnp.zeros_like(dq)
    aux = pack[2 * rows :, :].astype(F32)

    def step(j, carry):
        @pl.when(flag(j))
        def _():
            for h in range(heads):
                cols = slice(h * HEAD, (h + 1) * HEAD)
                part = lambda i: aux[(3 * i) * heads + h : (3 * i) * heads + h + 1] + (
                    aux[(3 * i + 1) * heads + h : (3 * i + 1) * heads + h + 1]
                    + aux[(3 * i + 2) * heads + h : (3 * i + 2) * heads + h + 1]
                )
                norm, delta = part(0) * LOG2E, part(1)
                q, g = pack[0:rows, cols], pack[rows : 2 * rows, cols]
                k, v = kv[j, 0:rows, cols], kv[j, rows : 2 * rows, cols]
                last = (((1,), (1,)), ((), ()))
                st = lax.dot_general(k, q, last, preferred_element_type=F32)
                p = jnp.exp2(st * (factor * LOG2E) - norm)
                dp = lax.dot_general(v, g, last, preferred_element_type=F32)
                ds = (p * (dp - delta)).astype(BF)
                acc[j, rows : 2 * rows, cols] += jnp.dot(p.astype(BF), g, preferred_element_type=F32)
                acc[j, 0:rows, cols] += jnp.dot(ds, q, preferred_element_type=F32)
                dq[:, cols] += lax.dot_general(ds, k, (((0,), (0,)), ((), ())), preferred_element_type=F32)

        return carry

    lax.fori_loop(0, count, step, 0)


def seen(extents, time_all, step, flip):
    time_pos, frame_pos = lax.axis_index("tm"), lax.axis_index("space")
    chip, core = frame_pos // 2, frame_pos % 2
    when = time_pos + step
    place = jnp.clip(when, 0, time_all - 1)
    if step == 0:
        cross, inner = jnp.bool_(False), jnp.bool_(False)
    else:
        edge = 0 if step < 0 else RING - 1
        cross, inner = time_pos % RING == edge, chip == (0 if step < 0 else 1)
    height = jnp.where(cross != bool(flip), 1 - chip, chip)
    extent = [extents[place, height * 2 + core, i] for i in range(3)]
    here = (when >= 0) & (when < time_all) & (abs(step) <= extent[0])

    def flag(j):
        key_height = jnp.where(j >= 2, 1 - chip, chip)
        taken = jnp.where(j >= 2, cross & inner, jnp.logical_not(cross) | inner)
        return here & taken & (jnp.abs(key_height - height) <= extent[1]) & (j % 2 <= extent[2])

    return flag


def frame_kernel(rows, factor, time_all, extents, mine, other, kv_a, kv_b, acc, dq_mine, dq_other, kv, dq):
    kv[0] = kv_a[...]
    kv[1] = kv_b[...]
    acc[...] = jnp.zeros_like(acc)
    accumulate(mine, seen(extents, time_all, 0, 0), 2, kv, acc, dq_mine, rows, factor)
    accumulate(other, seen(extents, time_all, 0, 1), 2, kv, acc, dq, rows, factor)
    dq_mine[...] = dq_mine[...] * factor
    dq_other[...] = (dq[...] * factor).astype(BF)


def near_kernel(rows, factor, time_all, extents, low, high, kv_a, kv_b, kv_c, kv_d, acc_in, acc, dq_low, dq_high, kv, dq):
    for i, ref in enumerate((kv_a, kv_b, kv_c, kv_d)):
        kv[i] = ref[...]
    acc[0:2] = acc_in[...]
    acc[2:4] = jnp.zeros_like(acc[2:4])
    accumulate(low, seen(extents, time_all, -1, 0), 4, kv, acc, dq, rows, factor)
    dq_low[...] = (dq[...] * factor).astype(BF)
    accumulate(high, seen(extents, time_all, 1, 0), 4, kv, acc, dq, rows, factor)
    dq_high[...] = (dq[...] * factor).astype(BF)


def far_kernel(rows, factor, time_all, extents, low, high, kv_a, kv_b, kv_c, kv_d, acc_in,
               dq_low, dq_high, own, lent, sib, kv, acc, dq):
    for i, ref in enumerate((kv_a, kv_b, kv_c, kv_d)):
        kv[i] = ref[...]
    acc[...] = acc_in[...]
    accumulate(low, seen(extents, time_all, -1, 1), 4, kv, acc, dq, rows, factor)
    dq_low[...] = (dq[...] * factor).astype(BF)
    accumulate(high, seen(extents, time_all, 1, 1), 4, kv, acc, dq, rows, factor)
    dq_high[...] = (dq[...] * factor).astype(BF)
    own[0:rows] = acc[0, 0:rows] * factor
    own[rows:] = acc[0, rows:]
    lent[0:rows] = acc[2, 0:rows] * factor
    lent[rows:] = acc[2, rows:]
    for i, j in enumerate((1, 3)):
        sib[i, 0:rows] = (acc[j, 0:rows] * factor).astype(BF)
        sib[i, rows:] = acc[j, rows:].astype(BF)


def call(kernel, shapes, scratch, operands, pairs, name):
    whole = pl.BlockSpec(memory_space=pltpu.VMEM)
    return pl.pallas_call(
        kernel,
        out_shape=shapes,
        in_specs=[pl.BlockSpec(memory_space=pltpu.SMEM)] + [whole] * (len(operands) - 1),
        out_specs=[whole] * len(shapes),
        scratch_shapes=scratch,
        compiler_params=pltpu.CompilerParams(vmem_limit_bytes=40 * 2**20),
        cost_estimate=pl.CostEstimate(flops=1000, bytes_accessed=1000, transcendentals=0),
        name=name,
    )(*operands)


def thirds(x):
    hi = lax.reduce_precision(x, 8, 7)
    mid = lax.reduce_precision(x - hi, 8, 7)
    return [hi.astype(BF), mid.astype(BF), (x - hi - mid).astype(BF)]


def body(query_tiles, key_tiles, value_tiles, grad_output, log_norm, row_delta, extents):
    rows, channels = query_tiles.shape[2:]
    heads = log_norm.shape[2]
    factor = (channels // heads) ** (-0.5)
    time_all = lax.axis_size("tm")
    route = routes(time_all)

    pad = jnp.zeros((32 - 6 * heads, channels), BF)
    mine = jnp.concatenate(
        [query_tiles[0, 0], grad_output[0, 0]] + thirds(log_norm[0, 0]) + thirds(row_delta[0, 0]) + [pad]
    )
    mine, key, value = lax.optimization_barrier((mine, key_tiles[0, 0], value_tiles[0, 0]))
    kv_a = jnp.concatenate([key, value])

    other = send(mine, route["pair"])
    near_low = send(mine, route["up"])
    near_high = send(mine, route["down"])
    kv_b = send(kv_a, route["core"])
    far_low = send(other, route["up"])
    far_high = send(other, route["down"])
    kv_c = send(lax.optimization_barrier((kv_a, kv_b, near_low, near_high))[0], route["lend"])

    tile, two = (rows, channels), (2 * rows, channels)
    out = jax.ShapeDtypeStruct
    with jax.named_scope("frame"):
        acc, dq_mine, dq_other = call(
            functools.partial(frame_kernel, rows, factor, time_all),
            [out((2,) + two, F32), out(tile, F32), out(tile, BF)],
            [pltpu.VMEM((2,) + two, BF), pltpu.VMEM(tile, F32)],
            (extents, mine, other, kv_a, kv_b), 4, "frame",
        )
    kv_c, dq_other = lax.optimization_barrier((kv_c, dq_other))
    kv_d = send(kv_c, route["lent_core"])
    with jax.named_scope("near"):
        acc, dq_low, dq_high = call(
            functools.partial(near_kernel, rows, factor, time_all),
            [out((4,) + two, F32), out(tile, BF), out(tile, BF)],
            [pltpu.VMEM((4,) + two, BF), pltpu.VMEM(tile, F32)],
            (extents, near_low, near_high, kv_a, kv_b, kv_c, kv_d, acc), 6, "near",
        )
    with jax.named_scope("far"):
        far_dq_low, far_dq_high, own, lent, sib = call(
            functools.partial(far_kernel, rows, factor, time_all),
            [out(tile, BF), out(tile, BF), out(two, F32), out(two, F32), out((2,) + two, BF)],
            [pltpu.VMEM((4,) + two, BF), pltpu.VMEM((4,) + two, F32), pltpu.VMEM(tile, F32)],
            (extents, far_low, far_high, kv_a, kv_b, kv_c, kv_d, acc), 6, "far",
        )
    parts = [
        send(dq_other, route["pair"]),
        send(dq_low, route["down"]),
        send(dq_high, route["up"]),
        send(far_dq_low, route["far_down"]),
        send(far_dq_high, route["far_up"]),
    ]
    sib = send(sib, route["core"])
    lent = (lent + sib[1].astype(F32)).astype(BF)
    given = send(lent, route["give"])
    total = dq_mine
    for part in parts:
        total = total + part.astype(F32)
    grad_kv = (own + sib[0].astype(F32) + given.astype(F32)).astype(BF)
    shape = (1, 1, rows, channels)
    return total.astype(BF).reshape(shape), grad_kv[:rows].reshape(shape), grad_kv[rows:].reshape(shape)


def solution(mesh):
    tiles, per_row = P("tm", "space", None, "heads"), P("tm", "space", "heads", None)
    return jax.shard_map(
        body,
        mesh=mesh,
        in_specs=(tiles, tiles, tiles, tiles, per_row, per_row, P()),
        out_specs=(tiles, tiles, tiles),
        check_vma=False,
    )
```

```python
import functools

import jax
import jax.numpy as jnp
from jax import lax
from jax.experimental import pallas as pl
from jax.experimental.pallas import tpu as pltpu
from jax.sharding import PartitionSpec as P

RING = 8
LOG2E = 1.4426950408889634
HEAD = 128
BF = jnp.bfloat16
F32 = jnp.float32


def send(block, pairs):
    return lax.ppermute(block, ("tm", "space"), pairs)


def routes(time_all):
    at = lambda t, c, w: t * 4 + c * 2 + w
    ts, cs = range(time_all), range(2)
    core = [(at(t, c, w), at(t, c, 1 - w)) for t in ts for c in cs for w in cs]
    pair = [(at(t, c, w), at(t, 1 - c, w)) for t in ts for c in cs for w in cs]
    up, lend, lent_core = [], [], []
    for t in range(time_all - 1):
        for w in cs:
            if t % RING == RING - 1:
                up.append((at(t, 1, w), at(t + 1, 0, w)))
                lend.append((at(t, 0, w), at(t, 1, w)))
                lend.append((at(t + 1, 1, w), at(t + 1, 0, w)))
                lent_core.append((at(t, 1, w), at(t, 1, 1 - w)))
                lent_core.append((at(t + 1, 0, w), at(t + 1, 0, 1 - w)))
            else:
                up += [(at(t, c, w), at(t + 1, c, w)) for c in cs]
    back = lambda pairs: [(j, i) for i, j in pairs]
    across = lambda pairs: [(j, i ^ 2) for i, j in pairs]
    return dict(
        core=core, pair=pair, up=up, down=back(up), lend=lend, lent_core=lent_core, give=back(lend),
        far_down=across(up), far_up=across(back(up)),
    )


def accumulate(pack, flag, count, kv, acc, dq, rows, factor):
    heads = pack.shape[1] // HEAD
    dq[...] = jnp.zeros_like(dq)
    aux = pack[2 * rows :, :].astype(F32)

    def step(j, carry):
        @pl.when(flag(j))
        def _():
            for h in range(heads):
                cols = slice(h * HEAD, (h + 1) * HEAD)
                part = lambda i: aux[(3 * i) * heads + h : (3 * i) * heads + h + 1] + (
                    aux[(3 * i + 1) * heads + h : (3 * i + 1) * heads + h + 1]
                    + aux[(3 * i + 2) * heads + h : (3 * i + 2) * heads + h + 1]
                )
                norm, delta = part(0) * LOG2E, part(1)
                q, g = pack[0:rows, cols], pack[rows : 2 * rows, cols]
                k, v = kv[j, 0:rows, cols], kv[j, rows : 2 * rows, cols]
                last = (((1,), (1,)), ((), ()))
                st = lax.dot_general(k, q, last, preferred_element_type=F32)
                p = jnp.exp2(st * (factor * LOG2E) - norm)
                dp = lax.dot_general(v, g, last, preferred_element_type=F32)
                ds = (p * (dp - delta)).astype(BF)
                acc[j, rows : 2 * rows, cols] += jnp.dot(p.astype(BF), g, preferred_element_type=F32)
                acc[j, 0:rows, cols] += jnp.dot(ds, q, preferred_element_type=F32)
                dq[:, cols] += lax.dot_general(ds, k, (((0,), (0,)), ((), ())), preferred_element_type=F32)

        return carry

    lax.fori_loop(0, count, step, 0)


def seen(extents, time_all, step, flip):
    time_pos, frame_pos = lax.axis_index("tm"), lax.axis_index("space")
    chip, core = frame_pos // 2, frame_pos % 2
    when = time_pos + step
    place = jnp.clip(when, 0, time_all - 1)
    if step == 0:
        cross, inner = jnp.bool_(False), jnp.bool_(False)
    else:
        edge = 0 if step < 0 else RING - 1
        cross, inner = time_pos % RING == edge, chip == (0 if step < 0 else 1)
    height = jnp.where(cross != bool(flip), 1 - chip, chip)
    extent = [extents[place, height * 2 + core, i] for i in range(3)]
    here = (when >= 0) & (when < time_all) & (abs(step) <= extent[0])

    def flag(j):
        key_height = jnp.where(j >= 2, 1 - chip, chip)
        taken = jnp.where(j >= 2, cross & inner, jnp.logical_not(cross) | inner)
        return here & taken & (jnp.abs(key_height - height) <= extent[1]) & (j % 2 <= extent[2])

    return flag


def pack_kernel(rows, query, grad, norm, delta, out, sems):
    copies = [pltpu.make_async_copy(r, out.at[pl.ds(i * rows, rows)], sems.at[i]) for i, r in enumerate((query, grad))]
    for copy in copies:
        copy.start()
    pieces = []
    for x in (norm[...], delta[...]):
        high = x.astype(BF)
        rest = x - high.astype(F32)
        mid = rest.astype(BF)
        pieces += [high.astype(F32), mid.astype(F32), rest - mid.astype(F32)]
    heads, channels = norm.shape
    pieces.append(jnp.zeros((32 - 6 * heads, channels), F32))
    out[2 * rows :] = jnp.concatenate(pieces).astype(BF)
    for copy in copies:
        copy.wait()


def stack_kernel(rows, key, value, out, sems):
    copies = [pltpu.make_async_copy(r, out.at[pl.ds(i * rows, rows)], sems.at[i]) for i, r in enumerate((key, value))]
    for copy in copies:
        copy.start()
    for copy in copies:
        copy.wait()


def own_kernel(rows, factor, time_all, extents, mine, kv_a, kv_b, acc, dq_mine, kv):
    kv[0] = kv_a[...]
    kv[1] = kv_b[...]
    acc[...] = jnp.zeros_like(acc)
    accumulate(mine, seen(extents, time_all, 0, 0), 2, kv, acc, dq_mine, rows, factor)
    dq_mine[...] = dq_mine[...] * factor


def pair_kernel(rows, factor, time_all, extents, other, kv_a, kv_b, acc_in, acc, dq_other, kv, dq):
    kv[0] = kv_a[...]
    kv[1] = kv_b[...]
    accumulate(other, seen(extents, time_all, 0, 1), 2, kv, acc, dq, rows, factor)
    dq_other[...] = (dq[...] * factor).astype(BF)


def near_kernel(rows, factor, time_all, extents, low, high, kv_a, kv_b, kv_c, kv_d, acc_in, acc, dq_low, dq_high, kv, dq):
    for i, ref in enumerate((kv_a, kv_b, kv_c, kv_d)):
        kv[i] = ref[...]
    accumulate(low, seen(extents, time_all, -1, 0), 4, kv, acc, dq, rows, factor)
    dq_low[...] = (dq[...] * factor).astype(BF)
    accumulate(high, seen(extents, time_all, 1, 0), 4, kv, acc, dq, rows, factor)
    dq_high[...] = (dq[...] * factor).astype(BF)


def far_kernel(rows, factor, time_all, extents, low, high, kv_a, kv_b, kv_c, kv_d, acc_in,
               dq_low, dq_high, own, lent, sib, kv, dq):
    for i, ref in enumerate((kv_a, kv_b, kv_c, kv_d)):
        kv[i] = ref[...]
    acc = acc_in
    accumulate(low, seen(extents, time_all, -1, 1), 4, kv, acc, dq, rows, factor)
    dq_low[...] = (dq[...] * factor).astype(BF)
    accumulate(high, seen(extents, time_all, 1, 1), 4, kv, acc, dq, rows, factor)
    dq_high[...] = (dq[...] * factor).astype(BF)
    own[0:rows] = acc[0, 0:rows] * factor
    own[rows:] = acc[0, rows:]
    lent[0:rows] = acc[2, 0:rows] * factor
    lent[rows:] = acc[2, rows:]
    for i, j in enumerate((1, 3)):
        sib[i, 0:rows] = (acc[j, 0:rows] * factor).astype(BF)
        sib[i, rows:] = acc[j, rows:].astype(BF)


def call(kernel, shapes, scratch, operands, micros, name, aliases=None):
    whole = pl.BlockSpec(memory_space=pltpu.VMEM)
    return pl.pallas_call(
        kernel,
        out_shape=shapes,
        in_specs=[pl.BlockSpec(memory_space=pltpu.SMEM)] + [whole] * (len(operands) - 1),
        out_specs=[whole] * len(shapes),
        scratch_shapes=scratch,
        input_output_aliases=aliases or {},
        compiler_params=pltpu.CompilerParams(vmem_limit_bytes=40 * 2**20),
        cost_estimate=pl.CostEstimate(flops=micros * 10**9 + 1000, bytes_accessed=1000, transcendentals=0),
        name=name,
    )(*operands)


def gathered(kernel, shape, blocks, rows, name):
    hbm, vmem = pl.BlockSpec(memory_space=pltpu.HBM), pl.BlockSpec(memory_space=pltpu.VMEM)
    return pl.pallas_call(
        functools.partial(kernel, rows),
        out_shape=shape,
        in_specs=[hbm] * 2 + [vmem] * (len(blocks) - 2),
        out_specs=vmem,
        scratch_shapes=[pltpu.SemaphoreType.DMA((2,))],
        cost_estimate=pl.CostEstimate(flops=10**9, bytes_accessed=1000, transcendentals=0),
        name=name,
    )(*blocks)


def body(query_tiles, key_tiles, value_tiles, grad_output, log_norm, row_delta, extents):
    rows, channels = query_tiles.shape[2:]
    heads = log_norm.shape[2]
    factor = (channels // heads) ** (-0.5)
    time_all = lax.axis_size("tm")
    route = routes(time_all)

    out = jax.ShapeDtypeStruct
    tile, two = (rows, channels), (2 * rows, channels)
    mine = gathered(
        pack_kernel, out((2 * rows + 32, channels), BF),
        (query_tiles[0, 0], grad_output[0, 0], log_norm[0, 0], row_delta[0, 0]), rows, "pack",
    )
    other = send(mine, route["pair"])
    mine, key, value = lax.optimization_barrier((mine, key_tiles[0, 0], value_tiles[0, 0]))
    kv_a = gathered(stack_kernel, out(two, BF), (key, value), rows, "stack")
    mine, kv_a = lax.optimization_barrier((mine, kv_a))
    kv_b = send(kv_a, route["core"])
    near_low = send(mine, route["up"])
    near_high = send(mine, route["down"])
    far_low = send(other, route["up"])
    far_high = send(other, route["down"])

    with jax.named_scope("own"):
        acc, dq_mine = call(
            functools.partial(own_kernel, rows, factor, time_all),
            [out((4,) + two, F32), out(tile, F32)],
            [pltpu.VMEM((2,) + two, BF)],
            (extents, mine, kv_a, kv_b), 0, "own",
        )
    kv_a, dq_mine, *_ = lax.optimization_barrier((kv_a, dq_mine, near_low, near_high, other))
    kv_c = send(kv_a, route["lend"])
    with jax.named_scope("other"):
        acc, dq_other = call(
            functools.partial(pair_kernel, rows, factor, time_all),
            [out((4,) + two, F32), out(tile, BF)],
            [pltpu.VMEM((2,) + two, BF), pltpu.VMEM(tile, F32)],
            (extents, other, kv_a, kv_b, acc), 0, "other", {4: 0},
        )
    kv_c, dq_other = lax.optimization_barrier((kv_c, dq_other))
    kv_d = send(kv_c, route["lent_core"])
    with jax.named_scope("near"):
        acc, dq_low, dq_high = call(
            functools.partial(near_kernel, rows, factor, time_all),
            [out((4,) + two, F32), out(tile, BF), out(tile, BF)],
            [pltpu.VMEM((4,) + two, BF), pltpu.VMEM(tile, F32)],
            (extents, near_low, near_high, kv_a, kv_b, kv_c, kv_d, acc), 0, "near", {7: 0},
        )
    with jax.named_scope("far"):
        far_dq_low, far_dq_high, own, lent, sib = call(
            functools.partial(far_kernel, rows, factor, time_all),
            [out(tile, BF), out(tile, BF), out(two, F32), out(two, F32), out((2,) + two, BF)],
            [pltpu.VMEM((4,) + two, BF), pltpu.VMEM(tile, F32)],
            (extents, far_low, far_high, kv_a, kv_b, kv_c, kv_d, acc), 20, "far",
        )
    early = [send(dq_other, route["pair"]), send(dq_low, route["down"]), send(dq_high, route["up"])]
    late = [send(far_dq_low, route["far_down"]), send(far_dq_high, route["far_up"])]
    sib, *early = lax.optimization_barrier((sib, *early))
    sib = send(sib, route["core"])
    lent = (lent + sib[1].astype(F32)).astype(BF)
    given = send(lent, route["give"])
    total = dq_mine
    for part in early + late:
        total = total + part.astype(F32)
    grad_kv = (own + sib[0].astype(F32) + given.astype(F32)).astype(BF)
    shape = (1, 1, rows, channels)
    return total.astype(BF).reshape(shape), grad_kv[:rows].reshape(shape), grad_kv[rows:].reshape(shape)


def solution(mesh):
    tiles, per_row = P("tm", "space", None, "heads"), P("tm", "space", "heads", None)
    return jax.shard_map(
        body,
        mesh=mesh,
        in_specs=(tiles, tiles, tiles, tiles, per_row, per_row, P()),
        out_specs=(tiles, tiles, tiles),
        check_vma=False,
    )
```

```python
import functools

import jax
import jax.numpy as jnp
from jax import lax
from jax.experimental import pallas as pl
from jax.experimental.pallas import tpu as pltpu
from jax.sharding import PartitionSpec as P

LOG2E = 1.4426950408889634
HEAD = 128
AUX = 32
NEVER = 1e30
BF = jnp.bfloat16
F32 = jnp.float32


def send(block, pairs):
    return lax.ppermute(block, ("tm", "space"), pairs)


def routes(time_all):
    at = lambda t, c, w: t * 4 + c * 2 + w
    every = [(t, c, w) for t in range(time_all) for c in range(2) for w in range(2)]
    near = {0: [], 1: []}
    for t, c, w in every:
        if t + 1 < time_all:
            near[t % 2] += [(at(t, c, w), at(t + 1, c, w)), (at(t + 1, c, w), at(t, c, w))]
    core = [(at(t, c, w), at(t, c, 1 - w)) for t, c, w in every]
    pair = [(at(t, c, w), at(t, 1 - c, w)) for t, c, w in every]
    return core, pair, near[0], near[1]


def pack_kernel(half, query, grad, norm, delta, pack, msg):
    chip = lax.axis_index("space") // 2
    rows = 2 * half
    keep = pl.ds(pl.multiple_of(chip * half, half), half)
    give = pl.ds(pl.multiple_of((1 - chip) * half, half), half)
    pack[0:half] = query[keep]
    pack[rows : rows + half] = grad[keep]
    msg[0:half] = query[give]
    msg[half:rows] = grad[give]
    pieces = []
    for ref in (norm, delta):
        x = ref[:, 0, :]
        high = x.astype(BF)
        rest = x - high.astype(F32)
        mid = rest.astype(BF)
        pieces += [high.astype(F32), mid.astype(F32), rest - mid.astype(F32)]
    heads, _, channels = norm.shape
    pieces.append(jnp.zeros((AUX - 6 * heads, channels), F32))
    aux = jnp.concatenate(pieces)
    turned = jnp.concatenate([aux[:, half:], aux[:, :half]], axis=1)
    aux = jnp.where(chip == 0, aux, turned).astype(BF)
    pack[2 * rows :] = aux
    msg[rows:] = aux


def join_kernel(half, msg, pack_in, pack):
    rows = 2 * half
    pack[half:rows] = msg[0:half]
    pack[rows + half : 2 * rows] = msg[half:rows]
    lane = lax.broadcasted_iota(jnp.int32, (AUX, pack.shape[1]), 1)
    own, got = pack_in[2 * rows :].astype(F32), msg[rows:].astype(F32)
    pack[2 * rows :] = jnp.where(lane < half, own, got).astype(BF)


def stack_kernel(rows, key, value, out):
    out[0:rows] = key[...]
    out[rows:] = value[...]


def seen(extents, time_all, step):
    time_pos, frame_pos = lax.axis_index("tm"), lax.axis_index("space")
    chip, core = frame_pos // 2, frame_pos % 2
    when = time_pos + step(time_pos)
    place = jnp.clip(when, 0, time_all - 1)
    inside = (when >= 0) & (when < time_all)
    gap = jnp.abs(when - time_pos)

    def flag(j, part):
        height = chip if part == 0 else 1 - chip
        extent = [extents[place, height * 2 + core, i] for i in range(3)]
        height_gap = jnp.where(j >= 2, 1 - part, part)
        return inside & (gap <= extent[0]) & (height_gap <= extent[1]) & (j % 2 <= extent[2])

    return flag


def accumulate(pack, flag, kv, acc, dq, factor):
    channels = pack.shape[1]
    rows = (pack.shape[0] - AUX) // 2
    heads = channels // HEAD
    dq[...] = jnp.zeros_like(dq)
    aux = pack[2 * rows :, :].astype(F32)
    first = lax.broadcasted_iota(jnp.int32, (1, rows), 1) < rows // 2
    last = (((1,), (1,)), ((), ()))

    def step(j, carry):
        own, other = flag(j, 0), flag(j, 1)

        @pl.when(own | other)
        def _():
            hide = jnp.where(first, jnp.where(own, 0.0, NEVER), jnp.where(other, 0.0, NEVER))
            for h in range(heads):
                cols = slice(h * HEAD, (h + 1) * HEAD)
                row = lambda i: aux[i * heads + h : i * heads + h + 1]
                norm = (row(0) + (row(1) + row(2))) * LOG2E + hide
                delta = row(3) + (row(4) + row(5))
                q, g = pack[0:rows, cols], pack[rows : 2 * rows, cols]
                k, v = kv[j, 0:rows, cols], kv[j, rows : 2 * rows, cols]
                st = lax.dot_general(k, q, last, preferred_element_type=F32)
                p = jnp.exp2(st * (factor * LOG2E) - norm)
                dp = lax.dot_general(v, g, last, preferred_element_type=F32)
                ds = (p * (dp - delta)).astype(BF)
                acc[j, rows : 2 * rows, cols] += jnp.dot(p.astype(BF), g, preferred_element_type=F32)
                acc[j, 0:rows, cols] += jnp.dot(ds, q, preferred_element_type=F32)
                dq[:, cols] += lax.dot_general(ds, k, (((0,), (0,)), ((), ())), preferred_element_type=F32)

        return carry

    lax.fori_loop(0, 4, step, 0)


def own_kernel(factor, time_all, extents, pack, kv_a, kv_b, kv_c, kv_d, acc, dq, kv):
    for i, ref in enumerate((kv_a, kv_b, kv_c, kv_d)):
        kv[i] = ref[...]
    acc[...] = jnp.zeros_like(acc)
    accumulate(pack, seen(extents, time_all, lambda t: 0), kv, acc, dq, factor)
    dq[...] = dq[...] * factor


def even_kernel(factor, time_all, extents, pack, kv, acc_in, acc, dq_out, dq):
    accumulate(pack, seen(extents, time_all, lambda t: 1 - 2 * (t % 2)), kv, acc, dq, factor)
    dq_out[...] = (dq[...] * factor).astype(BF)


def odd_kernel(factor, time_all, extents, pack, kv, acc, dq_out, own, lent, sib, dq):
    accumulate(pack, seen(extents, time_all, lambda t: 2 * (t % 2) - 1), kv, acc, dq, factor)
    dq_out[...] = (dq[...] * factor).astype(BF)
    rows = dq.shape[0]
    own[0:rows] = acc[0, 0:rows] * factor
    own[rows:] = acc[0, rows:]
    lent[0:rows] = acc[2, 0:rows] * factor
    lent[rows:] = acc[2, rows:]
    for i, j in enumerate((1, 3)):
        sib[i, 0:rows] = (acc[j, 0:rows] * factor).astype(BF)
        sib[i, rows:] = acc[j, rows:].astype(BF)


def sum_kernel(half, own, even, odd, mine, msg):
    total = own[...] + even[...].astype(F32) + odd[...].astype(F32)
    mine[...] = total[:half].astype(BF)
    msg[...] = total[half:].astype(BF)


def place_kernel(half, mine, got, out):
    chip = lax.axis_index("space") // 2
    out[pl.ds(pl.multiple_of(chip * half, half), half)] = mine[...]
    out[pl.ds(pl.multiple_of((1 - chip) * half, half), half)] = got[...]


def lend_kernel(lent, sib, out):
    out[...] = (lent[...] + sib[1].astype(F32)).astype(BF)


def close_kernel(rows, own, sib, given, key, value):
    total = own[...] + sib[0].astype(F32) + given[...].astype(F32)
    key[...] = total[:rows].astype(BF)
    value[...] = total[rows:].astype(BF)


def call(kernel, shapes, operands, micros, name, scratch=(), aliases=None, scalars=0):
    whole = pl.BlockSpec(memory_space=pltpu.VMEM)
    return pl.pallas_call(
        kernel,
        out_shape=shapes,
        in_specs=[pl.BlockSpec(memory_space=pltpu.SMEM)] * scalars + [whole] * (len(operands) - scalars),
        out_specs=[whole] * len(shapes),
        scratch_shapes=scratch,
        input_output_aliases=aliases or {},
        compiler_params=pltpu.CompilerParams(vmem_limit_bytes=40 * 2**20),
        cost_estimate=pl.CostEstimate(flops=micros * 10**9 + 1000, bytes_accessed=1000, transcendentals=0),
        name=name,
    )(*operands)


def body(query_tiles, key_tiles, value_tiles, grad_output, log_norm, row_delta, extents):
    rows, channels = query_tiles.shape[2:]
    heads, half = log_norm.shape[2], rows // 2
    factor = (channels // heads) ** (-0.5)
    time_all = lax.axis_size("tm")
    core, pair, even, odd = routes(time_all)
    out = jax.ShapeDtypeStruct
    tile, two = (rows, channels), (2 * rows, channels)

    pack, msg = call(
        functools.partial(pack_kernel, half),
        [out((2 * rows + AUX, channels), BF), out((rows + AUX, channels), BF)],
        (query_tiles[0, 0], grad_output[0, 0], log_norm.reshape(heads, 1, rows), row_delta.reshape(heads, 1, rows)),
        0, "pack",
    )
    msg = send(msg, pair)
    pack, key, value = lax.optimization_barrier((pack, key_tiles[0, 0], value_tiles[0, 0]))
    (kv_a,) = call(functools.partial(stack_kernel, rows), [out(two, BF)], (key, value), 0, "stack")
    kv_c = send(kv_a, pair)
    kv_b = send(kv_a, core)
    (pack,) = call(
        functools.partial(join_kernel, half), [out((2 * rows + AUX, channels), BF)], (msg, pack), 20, "join", aliases={1: 0}
    )
    odd_pack = send(pack, odd)
    even_pack = send(pack, even)
    kv_d = send(kv_c, core)

    with jax.named_scope("own"):
        acc, dq, kv = call(
            functools.partial(own_kernel, factor, time_all),
            [out((4,) + two, F32), out(tile, F32), out((4,) + two, BF)],
            (extents, pack, kv_a, kv_b, kv_c, kv_d), 0, "own", scalars=1,
        )
    with jax.named_scope("even"):
        acc, even_dq = call(
            functools.partial(even_kernel, factor, time_all),
            [out((4,) + two, F32), out(tile, BF)],
            (extents, even_pack, kv, acc), 0, "even", [pltpu.VMEM(tile, F32)], {3: 0}, scalars=1,
        )
    with jax.named_scope("odd"):
        odd_dq, own, lent, sib = call(
            functools.partial(odd_kernel, factor, time_all),
            [out(tile, BF), out(two, F32), out(two, F32), out((2,) + two, BF)],
            (extents, odd_pack, kv, acc), 20, "odd", [pltpu.VMEM(tile, F32)], scalars=1,
        )
    odd_back = send(odd_dq, odd)
    even_back = send(even_dq, even)
    sib, even_back = lax.optimization_barrier((sib, even_back))
    sib = send(sib, core)
    (lent,) = call(lend_kernel, [out(two, BF)], (lent, sib), 0, "lend")
    given = send(lent, pair)
    mine, msg = call(
        functools.partial(sum_kernel, half), [out((half, channels), BF)] * 2, (dq, even_back, odd_back), 20, "sum"
    )
    msg = send(msg, pair)
    (grad_query,) = call(functools.partial(place_kernel, half), [out(tile, BF)], (mine, msg), 0, "place")
    grad_key, grad_value = call(functools.partial(close_kernel, rows), [out(tile, BF)] * 2, (own, sib, given), 0, "close")
    shape = (1, 1, rows, channels)
    return grad_query.reshape(shape), grad_key.reshape(shape), grad_value.reshape(shape)


def solution(mesh):
    tiles, per_row = P("tm", "space", None, "heads"), P("tm", "space", "heads", None)
    return jax.shard_map(
        body,
        mesh=mesh,
        in_specs=(tiles, tiles, tiles, tiles, per_row, per_row, P()),
        out_specs=(tiles, tiles, tiles),
        check_vma=False,
    )
```

```python
import functools

import jax
import jax.numpy as jnp
from jax import lax
from jax.experimental import pallas as pl
from jax.experimental.pallas import tpu as pltpu
from jax.sharding import PartitionSpec as P

LOG2E = 1.4426950408889634
HEAD = 128
RING = 8
AUX = 32
NEVER = 1e30
BF = jnp.bfloat16
F32 = jnp.float32


def send(block, pairs):
    return lax.ppermute(block, ("tm", "space"), pairs)


def routes(time_all):
    at = lambda t, c, w: t * 4 + c * 2 + w
    every = [(t, c, w) for t in range(time_all) for c in range(2) for w in range(2)]
    both = lambda a, b: [(a, b), (b, a)]
    even, odd, cross, lift = [], [], [], []
    for t, c, w in every:
        if t + 1 >= time_all:
            continue
        if (t + 1) % RING:
            (odd if t % 2 else even).extend(both(at(t, c, w), at(t + 1, c, w)))
        elif c:
            cross += both(at(t, 1, w), at(t + 1, 0, w))
            lift += [(at(t, 0, w), at(t, 1, w)), (at(t + 1, 1, w), at(t + 1, 0, w))]
    core = [(at(t, c, w), at(t, c, 1 - w)) for t, c, w in every]
    pair = [(at(t, c, w), at(t, 1 - c, w)) for t, c, w in every]
    home = [(a, b ^ 2) for a, b in cross]
    return core, pair, even, odd, cross, lift, home


def position(time_all):
    time_pos, frame_pos = lax.axis_index("tm"), lax.axis_index("space")
    chip, core = frame_pos // 2, frame_pos % 2
    low = (time_pos % RING == 0) & (time_pos > 0)
    high = (time_pos % RING == RING - 1) & (time_pos < time_all - 1)
    return time_pos, chip, core, low | high, (low & (chip == 0)) | (high & (chip == 1))


def pack_kernel(half, query, grad, norm, delta, pack, msg, extra, whole, q, g, n, d, sems):
    copies = [pltpu.make_async_copy(a, b, sems.at[i]) for i, (a, b) in enumerate(((query, q), (grad, g), (norm, n), (delta, d)))]
    for copy in copies:
        copy.start()
    for copy in copies:
        copy.wait()
    chip = lax.axis_index("space") // 2
    rows = 2 * half
    keep = pl.ds(pl.multiple_of(chip * half, half), half)
    give = pl.ds(pl.multiple_of((1 - chip) * half, half), half)
    pieces = []
    for ref in (n, d):
        x = ref[:, 0, :]
        high = x.astype(BF)
        rest = x - high.astype(F32)
        mid = rest.astype(BF)
        pieces += [high.astype(F32), mid.astype(F32), rest - mid.astype(F32)]
    heads, _, channels = norm.shape
    pieces.append(jnp.zeros((AUX - 6 * heads, channels), F32))
    aux = jnp.concatenate(pieces)
    turned = jnp.concatenate([aux[:, half:], aux[:, :half]], axis=1)
    whole[2 * rows :] = aux.astype(BF)
    aux = jnp.where(chip == 0, aux, turned).astype(BF)
    whole[0:rows] = q[...]
    whole[rows : 2 * rows] = g[...]
    pack[0:half] = q[keep]
    pack[rows : rows + half] = g[keep]
    pack[2 * rows :] = aux
    msg[0:half] = q[give]
    msg[half:rows] = g[give]
    msg[rows:] = aux
    extra[0:half] = q[keep]
    extra[half:rows] = g[keep]
    extra[rows:] = aux


def join_kernel(half, msg, pack_in, pack):
    rows = 2 * half
    pack[0:half] = pack_in[0:half]
    pack[rows : rows + half] = pack_in[rows : rows + half]
    pack[half:rows] = msg[0:half]
    pack[rows + half : 2 * rows] = msg[half:rows]
    lane = lax.broadcasted_iota(jnp.int32, (AUX, pack.shape[1]), 1)
    own, got = pack_in[2 * rows :].astype(F32), msg[rows:].astype(F32)
    pack[2 * rows :] = jnp.where(lane < half, own, got).astype(BF)


def odd_join_kernel(half, time_all, msg, extra, pack, out):
    rows = 2 * half
    _, chip, _, _, inner = position(time_all)

    @pl.when(jnp.logical_not(inner))
    def _():
        out[...] = pack[...]

    @pl.when(inner)
    def _():
        for ref, part in ((msg, chip), (extra, 1 - chip)):
            out[pl.ds(pl.multiple_of(part * half, half), half)] = ref[0:half]
            out[pl.ds(pl.multiple_of(rows + part * half, half), half)] = ref[half:rows]
        aux = msg[rows:].astype(F32)
        turned = jnp.concatenate([aux[:, half:], aux[:, :half]], axis=1)
        out[2 * rows :] = jnp.where(chip == 1, aux, turned).astype(BF)


def stack_kernel(rows, key, value, out):
    out[0:rows] = key[...]
    out[rows:] = value[...]


def seen(extents, time_all, kind):
    time_pos, chip, core, end, inner = position(time_all)
    toward = 2 * (time_pos % 2) - 1
    when = time_pos + {"own": 0, "even": -toward, "odd": toward, "cross": toward}[kind]
    heights = [chip, 1 - chip]
    inside = (when >= 0) & (when < time_all)
    if kind == "odd":
        inside = inside & (jnp.logical_not(end) | inner)
        heights = [jnp.where(end, chip, height) for height in heights]
    if kind == "cross":
        inside = inside & inner
        heights = [1 - chip, 1 - chip]
    place = jnp.clip(when, 0, time_all - 1)
    gap = jnp.abs(when - time_pos)

    def flag(j, part):
        extent = [extents[place, heights[part] * 2 + core, i] for i in range(3)]
        height_gap = jnp.abs(jnp.where(j >= 2, 1 - chip, chip) - heights[part])
        return inside & (gap <= extent[0]) & (height_gap <= extent[1]) & (j % 2 <= extent[2])

    return flag


def row_terms(pack, rows, heads):
    aux = pack[2 * rows :, :].astype(F32)
    row = lambda i: aux[i * heads : (i + 1) * heads]
    return jnp.concatenate([(row(0) + (row(1) + row(2))) * LOG2E, row(3) + (row(4) + row(5))])


def hidden(own, other, rows):
    first = lax.broadcasted_iota(jnp.int32, (1, rows), 1) < rows // 2
    return jnp.where(first, jnp.where(own, 0.0, NEVER), jnp.where(other, 0.0, NEVER))


def pair_terms(q, g, k, v, norm, delta, factor):
    last, first = (((1,), (1,)), ((), ())), (((0,), (0,)), ((), ()))
    st = lax.dot_general(k, q, last, preferred_element_type=F32)
    p = jnp.exp2(st * (factor * LOG2E) - norm)
    dp = lax.dot_general(v, g, last, preferred_element_type=F32)
    ds = (p * (dp - delta)).astype(BF)
    value_term = jnp.dot(p.astype(BF), g, preferred_element_type=F32)
    key_term = jnp.dot(ds, q, preferred_element_type=F32)
    return lax.dot_general(ds, k, first, preferred_element_type=F32), key_term, value_term


def own_kernel(factor, time_all, extents, pack, kv_a, kv_b, acc, dq, kv):
    rows, channels = dq.shape
    heads = channels // HEAD
    kv[0] = kv_a[...]
    kv[1] = kv_b[...]
    acc[...] = jnp.zeros_like(acc)
    dq[...] = jnp.zeros_like(dq)
    flag = seen(extents, time_all, "own")
    terms = row_terms(pack, rows, heads)

    def step(j, carry):
        own, other = flag(j, 0), flag(j, 1)

        @pl.when(own | other)
        def _():
            hide = hidden(own, other, rows)
            for h in range(heads):
                cols = slice(h * HEAD, (h + 1) * HEAD)
                query_term, key_term, value_term = pair_terms(
                    pack[0:rows, cols], pack[rows : 2 * rows, cols], kv[j, 0:rows, cols], kv[j, rows:, cols],
                    terms[h : h + 1] + hide, terms[heads + h : heads + h + 1], factor,
                )
                dq[:, cols] += query_term
                acc[j, 0:rows, cols] += key_term
                acc[j, rows:, cols] += value_term

        return carry

    lax.fori_loop(0, 2, step, 0)


def frame_kernel(factor, time_all, extents, even, cross, own, kv_a, kv_b, kv_c, kv_d, acc_in, dq_in,
                 acc, dq_own, dq_even, dq_cross, kv, packs, terms, hide, dq):
    rows, channels = dq_own.shape
    heads = channels // HEAD
    for i, ref in enumerate((kv_a, kv_b, kv_c, kv_d)):
        kv[i] = ref[...]
    for i, ref in enumerate((even, cross, own)):
        packs[i] = ref[0 : 2 * rows]
        terms[i, 0 : 2 * heads] = row_terms(ref, rows, heads)
    acc[0:2] = acc_in[...]
    acc[2:4] = jnp.zeros_like(acc[2:4])
    dq[0:2] = jnp.zeros_like(dq[0:2])
    dq[2] = dq_in[...]
    see = [seen(extents, time_all, kind) for kind in ("even", "cross", "own")]

    def add(j, members):
        each = lambda pick, axis: jnp.concatenate([pick(m) for m in members], axis=axis) if len(members) > 1 else pick(members[0])
        for h in range(heads):
            cols = slice(h * HEAD, (h + 1) * HEAD)
            query_term, key_term, value_term = pair_terms(
                each(lambda m: packs[m, 0:rows, cols], 0), each(lambda m: packs[m, rows:, cols], 0),
                kv[j, 0:rows, cols], kv[j, rows:, cols],
                each(lambda m: terms[m, h : h + 1] + hide[m, 0:1], 1),
                each(lambda m: terms[m, heads + h : heads + h + 1], 1), factor,
            )
            for i, m in enumerate(members):
                dq[m, :, cols] += query_term[i * rows : (i + 1) * rows]
            acc[j, 0:rows, cols] += key_term
            acc[j, rows:, cols] += value_term

    def step(j, carry):
        on = []
        for i, flag in enumerate(see):
            parts = flag(j, 0), flag(j, 1)
            hide[i, 0:1] = hidden(*parts, rows)
            on.append(parts[0] | parts[1] if i < 2 else (parts[0] | parts[1]) & (j >= 2))
        count = sum(x.astype(jnp.int32) for x in on)
        one = jnp.where(on[0], 0, jnp.where(on[1], 1, 2))
        two = jnp.where(on[0] & on[1], 1, 2)

        @pl.when(count >= 2)
        def _():
            add(j, [one, two])

        @pl.when(count % 2 == 1)
        def _():
            add(j, [jnp.where(count == 3, 2, one)])

        return carry

    lax.fori_loop(0, 4, step, 0)
    dq_own[...] = dq[2] * factor
    dq_even[...] = (dq[0] * factor).astype(BF)
    dq_cross[...] = (dq[1] * factor).astype(BF)


def odd_kernel(factor, time_all, extents, pack, kv, acc_in, dq_out, own, lent, sib, acc, dq):
    rows, channels = dq.shape
    heads = channels // HEAD
    dq[...] = jnp.zeros_like(dq)
    flag = seen(extents, time_all, "odd")
    terms = row_terms(pack, rows, heads)

    def step(j, carry):
        first, second = flag(j, 0), flag(j, 1)

        @pl.when(jnp.logical_not(first | second))
        def _():
            acc[j] = acc_in[j]

        @pl.when(first | second)
        def _():
            hide = hidden(first, second, rows)
            for h in range(heads):
                cols = slice(h * HEAD, (h + 1) * HEAD)
                query_term, key_term, value_term = pair_terms(
                    pack[0:rows, cols], pack[rows : 2 * rows, cols], kv[j, 0:rows, cols], kv[j, rows:, cols],
                    terms[h : h + 1] + hide, terms[heads + h : heads + h + 1], factor,
                )
                dq[:, cols] += query_term
                acc[j, 0:rows, cols] = acc_in[j, 0:rows, cols] + key_term
                acc[j, rows:, cols] = acc_in[j, rows:, cols] + value_term

        return carry

    lax.fori_loop(0, 4, step, 0)
    dq_out[...] = (dq[...] * factor).astype(BF)
    own[0:rows] = acc[0, 0:rows] * factor
    own[rows:] = acc[0, rows:]
    lent[0:rows] = acc[2, 0:rows] * factor
    lent[rows:] = acc[2, rows:]
    for i, j in enumerate((1, 3)):
        sib[i, 0:rows] = (acc[j, 0:rows] * factor).astype(BF)
        sib[i, rows:] = acc[j, rows:].astype(BF)


def sum_kernel(half, own, even, odd, mine, msg):
    total = own[...] + even[...].astype(F32) + odd[...].astype(F32)
    mine[...] = total[:half]
    msg[...] = total[half:].astype(BF)


def settle_kernel(cross, far, out):
    out[...] = cross[...].astype(F32) + far[...].astype(F32)


def place_kernel(half, mine, got, ended, out):
    chip = lax.axis_index("space") // 2
    for ref, part in ((mine, chip), (got, 1 - chip)):
        at = pl.ds(pl.multiple_of(part * half, half), half)
        out[at] = (ref[...].astype(F32) + ended[at]).astype(BF)


def lend_kernel(lent, sib, out):
    out[...] = (lent[...] + sib[1].astype(F32)).astype(BF)


def close_kernel(rows, own, sib, given, key, value):
    total = own[...] + sib[0].astype(F32) + given[...].astype(F32)
    key[...] = total[:rows].astype(BF)
    value[...] = total[rows:].astype(BF)


def call(kernel, shapes, operands, micros, name, scratch=(), scalars=0):
    whole = pl.BlockSpec(memory_space=pltpu.VMEM)
    return pl.pallas_call(
        kernel,
        out_shape=shapes,
        in_specs=[pl.BlockSpec(memory_space=pltpu.SMEM)] * scalars + [whole] * (len(operands) - scalars),
        out_specs=[whole] * len(shapes),
        scratch_shapes=scratch,
        compiler_params=pltpu.CompilerParams(vmem_limit_bytes=24 * 2**20),
        cost_estimate=pl.CostEstimate(flops=micros * 10**9 + 1000, bytes_accessed=1000, transcendentals=0),
        name=name,
    )(*operands)


def body(query_tiles, key_tiles, value_tiles, grad_output, log_norm, row_delta, extents):
    rows, channels = query_tiles.shape[2:]
    heads, half = log_norm.shape[2], rows // 2
    factor = (channels // heads) ** (-0.5)
    time_all = lax.axis_size("tm")
    core, pair, even, odd, cross, lift, home = routes(time_all)
    out = jax.ShapeDtypeStruct
    tile, two, packet, part = (rows, channels), (2 * rows, channels), (2 * rows + AUX, channels), (rows + AUX, channels)
    lanes = (heads, 1, rows)

    pack, msg, extra, whole = pl.pallas_call(
        functools.partial(pack_kernel, half),
        out_shape=[out(packet, BF), out(part, BF), out(part, BF), out(packet, BF)],
        in_specs=[pl.BlockSpec(memory_space=pl.ANY)] * 4,
        out_specs=[pl.BlockSpec(memory_space=pltpu.VMEM)] * 4,
        scratch_shapes=[pltpu.VMEM(tile, BF)] * 2 + [pltpu.VMEM(lanes, F32)] * 2 + [pltpu.SemaphoreType.DMA((4,))],
        compiler_params=pltpu.CompilerParams(vmem_limit_bytes=60 * 2**20),
        cost_estimate=pl.CostEstimate(flops=1000, bytes_accessed=1000, transcendentals=0),
        name="pack",
    )(query_tiles[0, 0], grad_output[0, 0], log_norm.reshape(lanes), row_delta.reshape(lanes))
    msg = send(msg, pair)
    extra = send(extra, lift)
    whole = send(whole, cross)
    pack, key, value = lax.optimization_barrier((pack, key_tiles[0, 0], value_tiles[0, 0]))
    (kv_a,) = call(functools.partial(stack_kernel, rows), [out(two, BF)], (key, value), 0, "stack")
    kv_b = send(kv_a, core)
    kv_a, msg = lax.optimization_barrier((kv_a, msg))
    kv_c = send(kv_a, pair)
    (pack,) = call(functools.partial(join_kernel, half), [out(packet, BF)], (msg, pack), 20, "join")
    even_pack = send(pack, even)

    with jax.named_scope("own"):
        acc, dq = call(
            functools.partial(own_kernel, factor, time_all),
            [out((2,) + two, F32), out(tile, F32)],
            (extents, pack, kv_a, kv_b), 0, "own", [pltpu.VMEM((2,) + two, BF)], scalars=1,
        )
    extra, whole, dq = lax.optimization_barrier((extra, whole, dq))
    (odd_pack,) = call(functools.partial(odd_join_kernel, half, time_all), [out(packet, BF)], (msg, extra, pack), 100, "odd_join")
    odd_pack = send(odd_pack, odd + cross)
    kv_c, dq = lax.optimization_barrier((kv_c, dq))
    kv_d = send(kv_c, core)
    with jax.named_scope("frame"):
        acc, dq, even_dq, cross_dq, kv = call(
            functools.partial(frame_kernel, factor, time_all),
            [out((4,) + two, F32), out(tile, F32), out(tile, BF), out(tile, BF), out((4,) + two, BF)],
            (extents, even_pack, whole, pack, kv_a, kv_b, kv_c, kv_d, acc, dq), 0, "frame",
            [pltpu.VMEM((3,) + two, BF), pltpu.VMEM((3, 8, rows), F32), pltpu.VMEM((3, 8, rows), F32), pltpu.VMEM((3,) + tile, F32)],
            scalars=1,
        )
    with jax.named_scope("odd"):
        odd_dq, own, lent, sib = call(
            functools.partial(odd_kernel, factor, time_all),
            [out(tile, BF), out(two, F32), out(two, F32), out((2,) + two, BF)],
            (extents, odd_pack, kv, acc), 20, "odd", [pltpu.VMEM((4,) + two, F32), pltpu.VMEM(tile, F32)], scalars=1,
        )
    far_back = send(odd_dq, home)
    odd_back = send(odd_dq, odd)
    even_back = send(even_dq, even)
    cross_back = send(cross_dq, cross)
    sib, even_back, cross_back = lax.optimization_barrier((sib, even_back, cross_back))
    sib = send(sib, core)
    (lent,) = call(lend_kernel, [out(two, BF)], (lent, sib), 0, "lend")
    given = send(lent, pair)
    mine, msg = call(
        functools.partial(sum_kernel, half),
        [out((half, channels), F32), out((half, channels), BF)], (dq, even_back, odd_back), 20, "sum"
    )
    msg = send(msg, pair)
    (ended,) = call(settle_kernel, [out(tile, F32)], (cross_back, far_back), 100, "settle")
    (grad_query,) = call(functools.partial(place_kernel, half), [out(tile, BF)], (mine, msg, ended), 0, "place")
    grad_key, grad_value = call(functools.partial(close_kernel, rows), [out(tile, BF)] * 2, (own, sib, given), 0, "close")
    shape = (1, 1, rows, channels)
    return grad_query.reshape(shape), grad_key.reshape(shape), grad_value.reshape(shape)


def solution(mesh):
    tiles, per_row = P("tm", "space", None, "heads"), P("tm", "space", "heads", None)
    return jax.shard_map(
        body,
        mesh=mesh,
        in_specs=(tiles, tiles, tiles, tiles, per_row, per_row, P()),
        out_specs=(tiles, tiles, tiles),
        check_vma=False,
    )
```

```python
import functools

import jax
import jax.numpy as jnp
from jax import lax
from jax.experimental import pallas as pl
from jax.experimental.pallas import tpu as pltpu
from jax.sharding import PartitionSpec as P

LOG2E = 1.4426950408889634
HEAD = 128
RING = 8
AUX = 32
NEVER = 1e30
BF = jnp.bfloat16
F32 = jnp.float32


def send(block, pairs):
    return lax.ppermute(block, ("tm", "space"), pairs)


def routes(time_all):
    at = lambda t, c, w: t * 4 + c * 2 + w
    every = [(t, c, w) for t in range(time_all) for c in range(2) for w in range(2)]
    both = lambda a, b: [(a, b), (b, a)]
    even, odd, cross, lift = [], [], [], []
    for t, c, w in every:
        if t + 1 >= time_all:
            continue
        if (t + 1) % RING:
            (odd if t % 2 else even).extend(both(at(t, c, w), at(t + 1, c, w)))
        elif c:
            cross += both(at(t, 1, w), at(t + 1, 0, w))
            lift += [(at(t, 0, w), at(t, 1, w)), (at(t + 1, 1, w), at(t + 1, 0, w))]
    core = [(at(t, c, w), at(t, c, 1 - w)) for t, c, w in every]
    pair = [(at(t, c, w), at(t, 1 - c, w)) for t, c, w in every]
    home = [(a, b ^ 2) for a, b in cross]
    straight, diagonal = odd + home, [(a, b ^ 2) for a, b in odd] + home
    return core, pair, even, odd + cross, cross, lift, straight, diagonal


def position(time_all):
    time_pos, frame_pos = lax.axis_index("tm"), lax.axis_index("space")
    chip, core = frame_pos // 2, frame_pos % 2
    low = (time_pos % RING == 0) & (time_pos > 0)
    high = (time_pos % RING == RING - 1) & (time_pos < time_all - 1)
    return time_pos, chip, core, low | high, (low & (chip == 0)) | (high & (chip == 1))


def pack_kernel(half, query, grad, norm, delta, pack, msg, extra, whole, q, g, n, d, sems):
    copies = [pltpu.make_async_copy(a, b, sems.at[i]) for i, (a, b) in enumerate(((query, q), (grad, g), (norm, n), (delta, d)))]
    for copy in copies:
        copy.start()
    for copy in copies:
        copy.wait()
    chip = lax.axis_index("space") // 2
    rows = 2 * half
    keep = pl.ds(pl.multiple_of(chip * half, half), half)
    give = pl.ds(pl.multiple_of((1 - chip) * half, half), half)
    pieces = []
    for ref in (n, d):
        x = ref[:, 0, :]
        high = x.astype(BF)
        rest = x - high.astype(F32)
        mid = rest.astype(BF)
        pieces += [high.astype(F32), mid.astype(F32), rest - mid.astype(F32)]
    heads, _, channels = norm.shape
    pieces.append(jnp.zeros((AUX - 6 * heads, channels), F32))
    aux = jnp.concatenate(pieces)
    turned = jnp.concatenate([aux[:, half:], aux[:, :half]], axis=1)
    whole[2 * rows :] = aux.astype(BF)
    aux = jnp.where(chip == 0, aux, turned).astype(BF)
    whole[0:rows] = q[...]
    whole[rows : 2 * rows] = g[...]
    pack[0:half] = q[keep]
    pack[rows : rows + half] = g[keep]
    pack[2 * rows :] = aux
    msg[0:half] = q[give]
    msg[half:rows] = g[give]
    msg[rows:] = aux
    extra[0:half] = q[keep]
    extra[half:rows] = g[keep]
    extra[rows:] = aux


def join_kernel(half, msg, pack_in, pack):
    rows = 2 * half
    pack[0:half] = pack_in[0:half]
    pack[rows : rows + half] = pack_in[rows : rows + half]
    pack[half:rows] = msg[0:half]
    pack[rows + half : 2 * rows] = msg[half:rows]
    lane = lax.broadcasted_iota(jnp.int32, (AUX, pack.shape[1]), 1)
    own, got = pack_in[2 * rows :].astype(F32), msg[rows:].astype(F32)
    pack[2 * rows :] = jnp.where(lane < half, own, got).astype(BF)


def odd_join_kernel(half, time_all, msg, extra, pack, out):
    rows = 2 * half
    _, chip, _, _, inner = position(time_all)

    @pl.when(jnp.logical_not(inner))
    def _():
        out[...] = pack[...]

    @pl.when(inner)
    def _():
        for ref, part in ((msg, chip), (extra, 1 - chip)):
            out[pl.ds(pl.multiple_of(part * half, half), half)] = ref[0:half]
            out[pl.ds(pl.multiple_of(rows + part * half, half), half)] = ref[half:rows]
        aux = msg[rows:].astype(F32)
        turned = jnp.concatenate([aux[:, half:], aux[:, :half]], axis=1)
        out[2 * rows :] = jnp.where(chip == 1, aux, turned).astype(BF)


def stack_kernel(rows, key, value, out):
    out[0:rows] = key[...]
    out[rows:] = value[...]


def seen(extents, time_all, kind):
    time_pos, chip, core, end, inner = position(time_all)
    toward = 2 * (time_pos % 2) - 1
    when = time_pos + {"own": 0, "even": -toward, "odd": toward, "cross": toward}[kind]
    heights = [chip, 1 - chip]
    inside = (when >= 0) & (when < time_all)
    if kind == "odd":
        inside = inside & (jnp.logical_not(end) | inner)
        heights = [jnp.where(end, chip, height) for height in heights]
    if kind == "cross":
        inside = inside & inner
        heights = [1 - chip, 1 - chip]
    place = jnp.clip(when, 0, time_all - 1)
    gap = jnp.abs(when - time_pos)

    def flag(j, part):
        extent = [extents[place, heights[part] * 2 + core, i] for i in range(3)]
        height_gap = jnp.abs(jnp.where(j >= 2, 1 - chip, chip) - heights[part])
        return inside & (gap <= extent[0]) & (height_gap <= extent[1]) & (j % 2 <= extent[2])

    return flag


def row_terms(pack, rows, heads):
    aux = pack[2 * rows :, :].astype(F32)
    row = lambda i: aux[i * heads : (i + 1) * heads]
    return jnp.concatenate([(row(0) + (row(1) + row(2))) * LOG2E, row(3) + (row(4) + row(5))])


def hidden(own, other, rows):
    first = lax.broadcasted_iota(jnp.int32, (1, rows), 1) < rows // 2
    return jnp.where(first, jnp.where(own, 0.0, NEVER), jnp.where(other, 0.0, NEVER))


def pair_terms(q, g, k, v, norm, delta, factor):
    last, first = (((1,), (1,)), ((), ())), (((0,), (0,)), ((), ()))
    st = lax.dot_general(k, q, last, preferred_element_type=F32)
    p = jnp.exp2(st * (factor * LOG2E) - norm)
    dp = lax.dot_general(v, g, last, preferred_element_type=F32)
    ds = (p * (dp - delta)).astype(BF)
    value_term = jnp.dot(p.astype(BF), g, preferred_element_type=F32)
    key_term = jnp.dot(ds, q, preferred_element_type=F32)
    return lax.dot_general(ds, k, first, preferred_element_type=F32), key_term, value_term


def own_kernel(factor, time_all, extents, pack, kv_a, kv_b, acc, dq, kv):
    rows, channels = dq.shape
    heads = channels // HEAD
    kv[0] = kv_a[...]
    kv[1] = kv_b[...]
    acc[...] = jnp.zeros_like(acc)
    dq[...] = jnp.zeros_like(dq)
    flag = seen(extents, time_all, "own")
    terms = row_terms(pack, rows, heads)

    def step(j, carry):
        own, other = flag(j, 0), flag(j, 1)

        @pl.when(own | other)
        def _():
            hide = hidden(own, other, rows)
            for h in range(heads):
                cols = slice(h * HEAD, (h + 1) * HEAD)
                query_term, key_term, value_term = pair_terms(
                    pack[0:rows, cols], pack[rows : 2 * rows, cols], kv[j, 0:rows, cols], kv[j, rows:, cols],
                    terms[h : h + 1] + hide, terms[heads + h : heads + h + 1], factor,
                )
                dq[:, cols] += query_term
                acc[j, 0:rows, cols] += key_term
                acc[j, rows:, cols] += value_term

        return carry

    lax.fori_loop(0, 2, step, 0)


def frame_kernel(factor, time_all, extents, even, cross, own, kv_a, kv_b, kv_c, kv_d, acc_in, dq_in,
                 acc, dq_own, dq_even, dq_cross, kv, packs, terms, hide, dq):
    rows, channels = dq_own.shape
    heads = channels // HEAD
    for i, ref in enumerate((kv_a, kv_b, kv_c, kv_d)):
        kv[i] = ref[...]
    for i, ref in enumerate((even, cross, own)):
        packs[i] = ref[0 : 2 * rows]
        terms[i, 0 : 2 * heads] = row_terms(ref, rows, heads)
    acc[0:2] = acc_in[...]
    acc[2:4] = jnp.zeros_like(acc[2:4])
    dq[0:2] = jnp.zeros_like(dq[0:2])
    dq[2] = dq_in[...]
    see = [seen(extents, time_all, kind) for kind in ("even", "cross", "own")]

    def add(j, members):
        each = lambda pick, axis: jnp.concatenate([pick(m) for m in members], axis=axis) if len(members) > 1 else pick(members[0])
        for h in range(heads):
            cols = slice(h * HEAD, (h + 1) * HEAD)
            query_term, key_term, value_term = pair_terms(
                each(lambda m: packs[m, 0:rows, cols], 0), each(lambda m: packs[m, rows:, cols], 0),
                kv[j, 0:rows, cols], kv[j, rows:, cols],
                each(lambda m: terms[m, h : h + 1] + hide[m, 0:1], 1),
                each(lambda m: terms[m, heads + h : heads + h + 1], 1), factor,
            )
            for i, m in enumerate(members):
                dq[m, :, cols] += query_term[i * rows : (i + 1) * rows]
            acc[j, 0:rows, cols] += key_term
            acc[j, rows:, cols] += value_term

    def step(j, carry):
        on = []
        for i, flag in enumerate(see):
            parts = flag(j, 0), flag(j, 1)
            hide[i, 0:1] = hidden(*parts, rows)
            on.append(parts[0] | parts[1] if i < 2 else (parts[0] | parts[1]) & (j >= 2))
        count = sum(x.astype(jnp.int32) for x in on)
        one = jnp.where(on[0], 0, jnp.where(on[1], 1, 2))
        two = jnp.where(on[0] & on[1], 1, 2)

        @pl.when(count >= 2)
        def _():
            add(j, [one, two])

        @pl.when(count % 2 == 1)
        def _():
            add(j, [jnp.where(count == 3, 2, one)])

        return carry

    lax.fori_loop(0, 4, step, 0)
    dq_own[...] = dq[2] * factor
    dq_even[...] = (dq[0] * factor).astype(BF)
    dq_cross[...] = (dq[1] * factor).astype(BF)


def odd_kernel(factor, time_all, extents, pack, kv, acc_in, dq_straight, dq_diagonal, own, lent, sib, acc, dq):
    rows, channels = dq.shape
    heads = channels // HEAD
    dq[...] = jnp.zeros_like(dq)
    flag = seen(extents, time_all, "odd")
    terms = row_terms(pack, rows, heads)

    def step(j, carry):
        first, second = flag(j, 0), flag(j, 1)

        @pl.when(jnp.logical_not(first | second))
        def _():
            acc[j] = acc_in[j]

        @pl.when(first | second)
        def _():
            hide = hidden(first, second, rows)
            for h in range(heads):
                cols = slice(h * HEAD, (h + 1) * HEAD)
                query_term, key_term, value_term = pair_terms(
                    pack[0:rows, cols], pack[rows : 2 * rows, cols], kv[j, 0:rows, cols], kv[j, rows:, cols],
                    terms[h : h + 1] + hide, terms[heads + h : heads + h + 1], factor,
                )
                dq[:, cols] += query_term
                acc[j, 0:rows, cols] = acc_in[j, 0:rows, cols] + key_term
                acc[j, rows:, cols] = acc_in[j, rows:, cols] + value_term

        return carry

    lax.fori_loop(0, 4, step, 0)
    half = rows // 2
    _, chip, _, _, inner = position(time_all)
    turn = jnp.where(inner, chip, 0)
    for ref, part in ((dq_straight, turn), (dq_diagonal, 1 - turn)):
        ref[...] = (dq[pl.ds(pl.multiple_of(part * half, half), half)] * factor).astype(BF)
    own[0:rows] = acc[0, 0:rows] * factor
    own[rows:] = acc[0, rows:]
    lent[0:rows] = acc[2, 0:rows] * factor
    lent[rows:] = acc[2, rows:]
    for i, j in enumerate((1, 3)):
        sib[i, 0:rows] = (acc[j, 0:rows] * factor).astype(BF)
        sib[i, rows:] = acc[j, rows:].astype(BF)


def sum_kernel(half, own, even, mine, msg):
    total = own[...] + even[...].astype(F32)
    mine[...] = total[:half]
    msg[...] = total[half:].astype(BF)


def place_kernel(half, mine, got, straight, diagonal, cross, out):
    chip = lax.axis_index("space") // 2
    for ref, back, part in ((mine, straight, chip), (got, diagonal, 1 - chip)):
        at = pl.ds(pl.multiple_of(part * half, half), half)
        out[at] = (ref[...].astype(F32) + back[...].astype(F32) + cross[at].astype(F32)).astype(BF)


def lend_kernel(lent, sib, out):
    out[...] = (lent[...] + sib[1].astype(F32)).astype(BF)


def close_kernel(rows, own, sib, given, key, value):
    total = own[...] + sib[0].astype(F32) + given[...].astype(F32)
    key[...] = total[:rows].astype(BF)
    value[...] = total[rows:].astype(BF)


def call(kernel, shapes, operands, micros, name, scratch=(), scalars=0):
    whole = pl.BlockSpec(memory_space=pltpu.VMEM)
    return pl.pallas_call(
        kernel,
        out_shape=shapes,
        in_specs=[pl.BlockSpec(memory_space=pltpu.SMEM)] * scalars + [whole] * (len(operands) - scalars),
        out_specs=[whole] * len(shapes),
        scratch_shapes=scratch,
        compiler_params=pltpu.CompilerParams(vmem_limit_bytes=24 * 2**20),
        cost_estimate=pl.CostEstimate(flops=micros * 10**9 + 1000, bytes_accessed=1000, transcendentals=0),
        name=name,
    )(*operands)


def body(query_tiles, key_tiles, value_tiles, grad_output, log_norm, row_delta, extents):
    rows, channels = query_tiles.shape[2:]
    heads, half = log_norm.shape[2], rows // 2
    factor = (channels // heads) ** (-0.5)
    time_all = lax.axis_size("tm")
    core, pair, even, odd, cross, lift, straight, diagonal = routes(time_all)
    out = jax.ShapeDtypeStruct
    tile, two, packet, part = (rows, channels), (2 * rows, channels), (2 * rows + AUX, channels), (rows + AUX, channels)
    lanes = (heads, 1, rows)

    pack, msg, extra, whole = pl.pallas_call(
        functools.partial(pack_kernel, half),
        out_shape=[out(packet, BF), out(part, BF), out(part, BF), out(packet, BF)],
        in_specs=[pl.BlockSpec(memory_space=pl.ANY)] * 4,
        out_specs=[pl.BlockSpec(memory_space=pltpu.VMEM)] * 4,
        scratch_shapes=[pltpu.VMEM(tile, BF)] * 2 + [pltpu.VMEM(lanes, F32)] * 2 + [pltpu.SemaphoreType.DMA((4,))],
        compiler_params=pltpu.CompilerParams(vmem_limit_bytes=60 * 2**20),
        cost_estimate=pl.CostEstimate(flops=1000, bytes_accessed=1000, transcendentals=0),
        name="pack",
    )(query_tiles[0, 0], grad_output[0, 0], log_norm.reshape(lanes), row_delta.reshape(lanes))
    msg = send(msg, pair)
    extra = send(extra, lift)
    whole = send(whole, cross)
    (kv_a,) = call(functools.partial(stack_kernel, rows), [out(two, BF)], (key_tiles[0, 0], value_tiles[0, 0]), 0, "stack")
    kv_a, msg = lax.optimization_barrier((kv_a, msg))
    kv_b = send(kv_a, core)
    kv_c = send(kv_a, pair)
    (pack,) = call(functools.partial(join_kernel, half), [out(packet, BF)], (msg, pack), 20, "join")
    even_pack = send(pack, even)

    with jax.named_scope("own"):
        acc, dq = call(
            functools.partial(own_kernel, factor, time_all),
            [out((2,) + two, F32), out(tile, F32)],
            (extents, pack, kv_a, kv_b), 0, "own", [pltpu.VMEM((2,) + two, BF)], scalars=1,
        )
    extra, whole, dq = lax.optimization_barrier((extra, whole, dq))
    (odd_pack,) = call(functools.partial(odd_join_kernel, half, time_all), [out(packet, BF)], (msg, extra, pack), 100, "odd_join")
    odd_pack = send(odd_pack, odd)
    kv_c, dq = lax.optimization_barrier((kv_c, dq))
    kv_d = send(kv_c, core)
    with jax.named_scope("frame"):
        acc, dq, even_dq, cross_dq, kv = call(
            functools.partial(frame_kernel, factor, time_all),
            [out((4,) + two, F32), out(tile, F32), out(tile, BF), out(tile, BF), out((4,) + two, BF)],
            (extents, even_pack, whole, pack, kv_a, kv_b, kv_c, kv_d, acc, dq), 0, "frame",
            [pltpu.VMEM((3,) + two, BF), pltpu.VMEM((3, 8, rows), F32), pltpu.VMEM((3, 8, rows), F32), pltpu.VMEM((3,) + tile, F32)],
            scalars=1,
        )
    with jax.named_scope("odd"):
        straight_dq, diagonal_dq, own, lent, sib = call(
            functools.partial(odd_kernel, factor, time_all),
            [out((half, channels), BF)] * 2 + [out(two, F32), out(two, F32), out((2,) + two, BF)],
            (extents, odd_pack, kv, acc), 20, "odd", [pltpu.VMEM((4,) + two, F32), pltpu.VMEM(tile, F32)], scalars=1,
        )
    even_back = send(even_dq, even)
    sib, even_back = lax.optimization_barrier((sib, even_back))
    straight_back = send(straight_dq, straight)
    diagonal_back = send(diagonal_dq, diagonal)
    cross_back = send(cross_dq, cross)
    sib = send(sib, core)
    (lent,) = call(lend_kernel, [out(two, BF)], (lent, sib), 0, "lend")
    given = send(lent, pair)
    mine, msg = call(
        functools.partial(sum_kernel, half), [out((half, channels), F32), out((half, channels), BF)], (dq, even_back), 0, "sum"
    )
    msg = send(msg, pair)
    (grad_query,) = call(
        functools.partial(place_kernel, half), [out(tile, BF)], (mine, msg, straight_back, diagonal_back, cross_back), 0, "place"
    )
    grad_key, grad_value = call(functools.partial(close_kernel, rows), [out(tile, BF)] * 2, (own, sib, given), 0, "close")
    shape = (1, 1, rows, channels)
    return grad_query.reshape(shape), grad_key.reshape(shape), grad_value.reshape(shape)


def solution(mesh):
    tiles, per_row = P("tm", "space", None, "heads"), P("tm", "space", "heads", None)
    return jax.shard_map(
        body,
        mesh=mesh,
        in_specs=(tiles, tiles, tiles, tiles, per_row, per_row, P()),
        out_specs=(tiles, tiles, tiles),
        check_vma=False,
    )
```

```python
import functools

import jax
import jax.numpy as jnp
from jax import lax
from jax.experimental import pallas as pl
from jax.experimental.pallas import tpu as pltpu
from jax.sharding import PartitionSpec as P

LOG2E = 1.4426950408889634
HEAD = 128
RING = 8
AUX = 32
NEVER = 1e30
BF = jnp.bfloat16
F32 = jnp.float32


def send(block, pairs):
    return lax.ppermute(block, ("tm", "space"), pairs)


def routes(time_all):
    at = lambda t, c, w: t * 4 + c * 2 + w
    every = [(t, c, w) for t in range(time_all) for c in range(2) for w in range(2)]
    both = lambda a, b: [(a, b), (b, a)]
    even, odd, cross, lift = [], [], [], []
    for t, c, w in every:
        if t + 1 >= time_all:
            continue
        if (t + 1) % RING:
            (odd if t % 2 else even).extend(both(at(t, c, w), at(t + 1, c, w)))
        elif c:
            cross += both(at(t, 1, w), at(t + 1, 0, w))
            lift += [(at(t, 0, w), at(t, 1, w)), (at(t + 1, 1, w), at(t + 1, 0, w))]
    core = [(at(t, c, w), at(t, c, 1 - w)) for t, c, w in every]
    pair = [(at(t, c, w), at(t, 1 - c, w)) for t, c, w in every]
    home = [(a, b ^ 2) for a, b in cross]
    straight, diagonal = odd + home, [(a, b ^ 2) for a, b in odd] + home
    return core, pair, even, odd + cross, cross, lift, straight, diagonal


def position(time_all):
    time_pos, frame_pos = lax.axis_index("tm"), lax.axis_index("space")
    chip, core = frame_pos // 2, frame_pos % 2
    low = (time_pos % RING == 0) & (time_pos > 0)
    high = (time_pos % RING == RING - 1) & (time_pos < time_all - 1)
    return time_pos, chip, core, low | high, (low & (chip == 0)) | (high & (chip == 1))


def pack_kernel(half, query, grad, norm, delta, pack, msg, extra, whole, q, g, n, d, sems):
    copies = [pltpu.make_async_copy(a, b, sems.at[i]) for i, (a, b) in enumerate(((query, q), (grad, g), (norm, n), (delta, d)))]
    for copy in copies:
        copy.start()
    for copy in copies:
        copy.wait()
    chip = lax.axis_index("space") // 2
    rows = 2 * half
    keep = pl.ds(pl.multiple_of(chip * half, half), half)
    give = pl.ds(pl.multiple_of((1 - chip) * half, half), half)
    pieces = []
    for ref in (n, d):
        x = ref[:, 0, :]
        high = x.astype(BF)
        rest = x - high.astype(F32)
        mid = rest.astype(BF)
        pieces += [high.astype(F32), mid.astype(F32), rest - mid.astype(F32)]
    heads, _, channels = norm.shape
    pieces.append(jnp.zeros((AUX - 6 * heads, channels), F32))
    aux = jnp.concatenate(pieces)
    turned = jnp.concatenate([aux[:, half:], aux[:, :half]], axis=1)
    whole[2 * rows :] = aux.astype(BF)
    aux = jnp.where(chip == 0, aux, turned).astype(BF)
    whole[0:rows] = q[...]
    whole[rows : 2 * rows] = g[...]
    pack[0:half] = q[keep]
    pack[rows : rows + half] = g[keep]
    pack[2 * rows :] = aux
    msg[0:half] = q[give]
    msg[half:rows] = g[give]
    msg[rows:] = aux
    extra[0:half] = q[keep]
    extra[half:rows] = g[keep]
    extra[rows:] = aux


def join_kernel(half, msg, pack_in, pack):
    rows = 2 * half
    pack[0:half] = pack_in[0:half]
    pack[rows : rows + half] = pack_in[rows : rows + half]
    pack[half:rows] = msg[0:half]
    pack[rows + half : 2 * rows] = msg[half:rows]
    lane = lax.broadcasted_iota(jnp.int32, (AUX, pack.shape[1]), 1)
    own, got = pack_in[2 * rows :].astype(F32), msg[rows:].astype(F32)
    pack[2 * rows :] = jnp.where(lane < half, own, got).astype(BF)


def odd_join_kernel(half, time_all, msg, extra, pack, out):
    rows = 2 * half
    _, chip, _, _, inner = position(time_all)

    @pl.when(jnp.logical_not(inner))
    def _():
        out[...] = pack[...]

    @pl.when(inner)
    def _():
        for ref, part in ((msg, chip), (extra, 1 - chip)):
            out[pl.ds(pl.multiple_of(part * half, half), half)] = ref[0:half]
            out[pl.ds(pl.multiple_of(rows + part * half, half), half)] = ref[half:rows]
        aux = msg[rows:].astype(F32)
        turned = jnp.concatenate([aux[:, half:], aux[:, :half]], axis=1)
        out[2 * rows :] = jnp.where(chip == 1, aux, turned).astype(BF)


def stack_kernel(rows, key, value, out):
    out[0:rows] = key[...]
    out[rows:] = value[...]


def seen(extents, time_all, kind):
    time_pos, chip, core, end, inner = position(time_all)
    toward = 2 * (time_pos % 2) - 1
    when = time_pos + {"own": 0, "even": -toward, "odd": toward, "cross": toward}[kind]
    heights = [chip, 1 - chip]
    inside = (when >= 0) & (when < time_all)
    if kind == "odd":
        inside = inside & (jnp.logical_not(end) | inner)
        heights = [jnp.where(end, chip, height) for height in heights]
    if kind == "cross":
        inside = inside & inner
        heights = [1 - chip, 1 - chip]
    place = jnp.clip(when, 0, time_all - 1)
    gap = jnp.abs(when - time_pos)

    def flag(j, part):
        extent = [extents[place, heights[part] * 2 + core, i] for i in range(3)]
        height_gap = jnp.abs(jnp.where(j >= 2, 1 - chip, chip) - heights[part])
        return inside & (gap <= extent[0]) & (height_gap <= extent[1]) & (j % 2 <= extent[2])

    return flag


def row_terms(pack, rows, heads):
    aux = pack[2 * rows :, :].astype(F32)
    row = lambda i: aux[i * heads : (i + 1) * heads]
    return jnp.concatenate([(row(0) + (row(1) + row(2))) * LOG2E, row(3) + (row(4) + row(5))])


def hidden(own, other, rows):
    first = lax.broadcasted_iota(jnp.int32, (1, rows), 1) < rows // 2
    return jnp.where(first, jnp.where(own, 0.0, NEVER), jnp.where(other, 0.0, NEVER))


def pair_terms(q, g, k, v, norm, delta, factor):
    last, first = (((1,), (1,)), ((), ())), (((0,), (0,)), ((), ()))
    st = lax.dot_general(k, q, last, preferred_element_type=F32)
    p = jnp.exp2(st * (factor * LOG2E) - norm)
    dp = lax.dot_general(v, g, last, preferred_element_type=F32)
    ds = (p * (dp - delta)).astype(BF)
    value_term = jnp.dot(p.astype(BF), g, preferred_element_type=F32)
    key_term = jnp.dot(ds, q, preferred_element_type=F32)
    return lax.dot_general(ds, k, first, preferred_element_type=F32), key_term, value_term


def own_kernel(factor, time_all, extents, pack, kv_a, kv_b, acc, dq, kv):
    rows, channels = dq.shape
    heads = channels // HEAD
    kv[0] = kv_a[...]
    kv[1] = kv_b[...]
    acc[...] = jnp.zeros_like(acc)
    dq[...] = jnp.zeros_like(dq)
    flag = seen(extents, time_all, "own")
    terms = row_terms(pack, rows, heads)

    def step(j, carry):
        own, other = flag(j, 0), flag(j, 1)

        @pl.when(own | other)
        def _():
            hide = hidden(own, other, rows)
            for h in range(heads):
                cols = slice(h * HEAD, (h + 1) * HEAD)
                query_term, key_term, value_term = pair_terms(
                    pack[0:rows, cols], pack[rows : 2 * rows, cols], kv[j, 0:rows, cols], kv[j, rows:, cols],
                    terms[h : h + 1] + hide, terms[heads + h : heads + h + 1], factor,
                )
                dq[:, cols] += query_term
                acc[j, 0:rows, cols] += key_term
                acc[j, rows:, cols] += value_term

        return carry

    lax.fori_loop(0, 2, step, 0)


def frame_kernel(factor, time_all, extents, even, cross, own, kv_a, kv_b, kv_c, kv_d, acc_in, dq_in,
                 acc, dq_own, dq_even, dq_cross, kv, packs, terms, dq, order):
    rows, channels = dq_own.shape
    heads, half = channels // HEAD, rows // 2
    for i, ref in enumerate((kv_a, kv_b, kv_c, kv_d)):
        kv[i] = ref[...]
    for i, ref in enumerate((even, cross, own)):
        each = row_terms(ref, rows, heads)
        for part in range(2):
            packs[2 * i + part, 0:half] = ref[part * half : (part + 1) * half]
            packs[2 * i + part, half:rows] = ref[rows + part * half : rows + (part + 1) * half]
            terms[2 * i + part, 0 : 2 * heads] = each[:, part * half : (part + 1) * half]
    acc[0:2] = acc_in[...]
    acc[2:4] = jnp.zeros_like(acc[2:4])
    dq[0:4] = jnp.zeros_like(dq[0:4])
    dq[4] = dq_in[0:half]
    dq[5] = dq_in[half:]
    see = [seen(extents, time_all, kind) for kind in ("even", "cross", "own")]

    def add(j, start, size, count):
        members = [order[start + i] for i in range(size)]
        hide = [jnp.where(start + i < count, 0.0, NEVER) for i in range(size)]
        each = lambda pick, axis: jnp.concatenate([pick(i, m) for i, m in enumerate(members)], axis=axis)
        for h in range(heads):
            cols = slice(h * HEAD, (h + 1) * HEAD)
            query_term, key_term, value_term = pair_terms(
                each(lambda i, m: packs[m, 0:half, cols], 0), each(lambda i, m: packs[m, half:rows, cols], 0),
                kv[j, 0:rows, cols], kv[j, rows:, cols],
                each(lambda i, m: terms[m, h : h + 1] + hide[i], 1),
                each(lambda i, m: terms[m, heads + h : heads + h + 1], 1), factor,
            )
            for i, m in enumerate(members):
                dq[m, :, cols] += query_term[i * half : (i + 1) * half]
            acc[j, 0:rows, cols] += key_term
            acc[j, rows:, cols] += value_term

    def step(j, carry):
        for i in range(6):
            order[i] = 0
        count = jnp.int32(0)
        for i, flag in enumerate(see):
            for part in range(2):
                on = flag(j, part) if i < 2 else flag(j, part) & (j >= 2)

                @pl.when(on)
                def _(unit=2 * i + part, count=count):
                    order[count] = unit

                count = count + on.astype(jnp.int32)

        @pl.when(count >= 3)
        def _():
            add(j, 0, 4, count)

        @pl.when((count > 4) | ((count > 0) & (count < 3)))
        def _():
            add(j, jnp.where(count > 4, 4, 0), 2, count)

        return carry

    lax.fori_loop(0, 4, step, 0)
    for part in range(2):
        at = slice(part * half, (part + 1) * half)
        dq_even[at] = (dq[part] * factor).astype(BF)
        dq_cross[at] = (dq[2 + part] * factor).astype(BF)
        dq_own[at] = dq[4 + part] * factor


def odd_kernel(factor, time_all, extents, pack, kv, acc_in, dq_straight, dq_diagonal, own, lent, sib, acc, dq):
    rows, channels = dq.shape
    heads = channels // HEAD
    dq[...] = jnp.zeros_like(dq)
    flag = seen(extents, time_all, "odd")
    terms = row_terms(pack, rows, heads)

    def step(j, carry):
        first, second = flag(j, 0), flag(j, 1)

        @pl.when(jnp.logical_not(first | second))
        def _():
            acc[j] = acc_in[j]

        @pl.when(first | second)
        def _():
            hide = hidden(first, second, rows)
            for h in range(heads):
                cols = slice(h * HEAD, (h + 1) * HEAD)
                query_term, key_term, value_term = pair_terms(
                    pack[0:rows, cols], pack[rows : 2 * rows, cols], kv[j, 0:rows, cols], kv[j, rows:, cols],
                    terms[h : h + 1] + hide, terms[heads + h : heads + h + 1], factor,
                )
                dq[:, cols] += query_term
                acc[j, 0:rows, cols] = acc_in[j, 0:rows, cols] + key_term
                acc[j, rows:, cols] = acc_in[j, rows:, cols] + value_term

        return carry

    lax.fori_loop(0, 4, step, 0)
    half = rows // 2
    _, chip, _, _, inner = position(time_all)
    turn = jnp.where(inner, chip, 0)
    for ref, part in ((dq_straight, turn), (dq_diagonal, 1 - turn)):
        ref[...] = (dq[pl.ds(pl.multiple_of(part * half, half), half)] * factor).astype(BF)
    own[0:rows] = acc[0, 0:rows] * factor
    own[rows:] = acc[0, rows:]
    lent[0:rows] = acc[2, 0:rows] * factor
    lent[rows:] = acc[2, rows:]
    for i, j in enumerate((1, 3)):
        sib[i, 0:rows] = (acc[j, 0:rows] * factor).astype(BF)
        sib[i, rows:] = acc[j, rows:].astype(BF)


def sum_kernel(half, own, even, mine, msg):
    total = own[...] + even[...].astype(F32)
    mine[...] = total[:half]
    msg[...] = total[half:].astype(BF)


def place_kernel(half, mine, got, straight, diagonal, cross, out):
    chip = lax.axis_index("space") // 2
    for ref, back, part in ((mine, straight, chip), (got, diagonal, 1 - chip)):
        at = pl.ds(pl.multiple_of(part * half, half), half)
        out[at] = (ref[...].astype(F32) + back[...].astype(F32) + cross[at].astype(F32)).astype(BF)


def lend_kernel(lent, sib, out):
    out[...] = (lent[...] + sib[1].astype(F32)).astype(BF)


def close_kernel(rows, own, sib, given, key, value):
    total = own[...] + sib[0].astype(F32) + given[...].astype(F32)
    key[...] = total[:rows].astype(BF)
    value[...] = total[rows:].astype(BF)


def call(kernel, shapes, operands, micros, name, scratch=(), scalars=0):
    whole = pl.BlockSpec(memory_space=pltpu.VMEM)
    return pl.pallas_call(
        kernel,
        out_shape=shapes,
        in_specs=[pl.BlockSpec(memory_space=pltpu.SMEM)] * scalars + [whole] * (len(operands) - scalars),
        out_specs=[whole] * len(shapes),
        scratch_shapes=scratch,
        compiler_params=pltpu.CompilerParams(vmem_limit_bytes=24 * 2**20),
        cost_estimate=pl.CostEstimate(flops=micros * 10**9 + 1000, bytes_accessed=1000, transcendentals=0),
        name=name,
    )(*operands)


def body(query_tiles, key_tiles, value_tiles, grad_output, log_norm, row_delta, extents):
    rows, channels = query_tiles.shape[2:]
    heads, half = log_norm.shape[2], rows // 2
    factor = (channels // heads) ** (-0.5)
    time_all = lax.axis_size("tm")
    core, pair, even, odd, cross, lift, straight, diagonal = routes(time_all)
    out = jax.ShapeDtypeStruct
    tile, two, packet, part = (rows, channels), (2 * rows, channels), (2 * rows + AUX, channels), (rows + AUX, channels)
    lanes = (heads, 1, rows)

    pack, msg, extra, whole = pl.pallas_call(
        functools.partial(pack_kernel, half),
        out_shape=[out(packet, BF), out(part, BF), out(part, BF), out(packet, BF)],
        in_specs=[pl.BlockSpec(memory_space=pl.ANY)] * 4,
        out_specs=[pl.BlockSpec(memory_space=pltpu.VMEM)] * 4,
        scratch_shapes=[pltpu.VMEM(tile, BF)] * 2 + [pltpu.VMEM(lanes, F32)] * 2 + [pltpu.SemaphoreType.DMA((4,))],
        compiler_params=pltpu.CompilerParams(vmem_limit_bytes=60 * 2**20),
        cost_estimate=pl.CostEstimate(flops=1000, bytes_accessed=1000, transcendentals=0),
        name="pack",
    )(query_tiles[0, 0], grad_output[0, 0], log_norm.reshape(lanes), row_delta.reshape(lanes))
    msg = send(msg, pair)
    extra = send(extra, lift)
    whole = send(whole, cross)
    (kv_a,) = call(functools.partial(stack_kernel, rows), [out(two, BF)], (key_tiles[0, 0], value_tiles[0, 0]), 0, "stack")
    kv_a, msg = lax.optimization_barrier((kv_a, msg))
    kv_b = send(kv_a, core)
    kv_c = send(kv_a, pair)
    (pack,) = call(functools.partial(join_kernel, half), [out(packet, BF)], (msg, pack), 20, "join")
    even_pack = send(pack, even)

    with jax.named_scope("own"):
        acc, dq = call(
            functools.partial(own_kernel, factor, time_all),
            [out((2,) + two, F32), out(tile, F32)],
            (extents, pack, kv_a, kv_b), 0, "own", [pltpu.VMEM((2,) + two, BF)], scalars=1,
        )
    extra, whole, dq = lax.optimization_barrier((extra, whole, dq))
    (odd_pack,) = call(functools.partial(odd_join_kernel, half, time_all), [out(packet, BF)], (msg, extra, pack), 100, "odd_join")
    odd_pack = send(odd_pack, odd)
    kv_c, dq = lax.optimization_barrier((kv_c, dq))
    kv_d = send(kv_c, core)
    with jax.named_scope("frame"):
        acc, dq, even_dq, cross_dq, kv = call(
            functools.partial(frame_kernel, factor, time_all),
            [out((4,) + two, F32), out(tile, F32), out(tile, BF), out(tile, BF), out((4,) + two, BF)],
            (extents, even_pack, whole, pack, kv_a, kv_b, kv_c, kv_d, acc, dq), 0, "frame",
            [pltpu.VMEM((6,) + tile, BF), pltpu.VMEM((6, 8, half), F32), pltpu.VMEM((6, half, channels), F32), pltpu.SMEM((8,), jnp.int32)],
            scalars=1,
        )
    with jax.named_scope("odd"):
        straight_dq, diagonal_dq, own, lent, sib = call(
            functools.partial(odd_kernel, factor, time_all),
            [out((half, channels), BF)] * 2 + [out(two, F32), out(two, F32), out((2,) + two, BF)],
            (extents, odd_pack, kv, acc), 20, "odd", [pltpu.VMEM((4,) + two, F32), pltpu.VMEM(tile, F32)], scalars=1,
        )
    even_back = send(even_dq, even)
    sib, even_back = lax.optimization_barrier((sib, even_back))
    straight_back = send(straight_dq, straight)
    diagonal_back = send(diagonal_dq, diagonal)
    cross_back = send(cross_dq, cross)
    sib = send(sib, core)
    (lent,) = call(lend_kernel, [out(two, BF)], (lent, sib), 0, "lend")
    given = send(lent, pair)
    mine, msg = call(
        functools.partial(sum_kernel, half), [out((half, channels), F32), out((half, channels), BF)], (dq, even_back), 0, "sum"
    )
    msg = send(msg, pair)
    (grad_query,) = call(
        functools.partial(place_kernel, half), [out(tile, BF)], (mine, msg, straight_back, diagonal_back, cross_back), 0, "place"
    )
    grad_key, grad_value = call(functools.partial(close_kernel, rows), [out(tile, BF)] * 2, (own, sib, given), 0, "close")
    shape = (1, 1, rows, channels)
    return grad_query.reshape(shape), grad_key.reshape(shape), grad_value.reshape(shape)


def solution(mesh):
    tiles, per_row = P("tm", "space", None, "heads"), P("tm", "space", "heads", None)
    return jax.shard_map(
        body,
        mesh=mesh,
        in_specs=(tiles, tiles, tiles, tiles, per_row, per_row, P()),
        out_specs=(tiles, tiles, tiles),
        check_vma=False,
    )
```
